32 devices in a mesh: rep: 4 (over y, x), exp: 8 (over z, core).
Axes of the slice: x: 2, y: 2, z: 4, core: 2. Of those that a mesh axis runs over, the one named last changes fastest.
Arguments:
- features: bfloat16 [4096, 2048], P(('rep', 'exp')), may hold values from -6 to 6
- out_grad: bfloat16 [4096, 2048], P(('rep', 'exp')), may hold values from -1.5 to 1.5
- expert_ids: int32 [4096, 2], P(('rep', 'exp')), may hold values from 0 to 7, all different within a row; in each aligned block of 128 rows (0 to 127, 128 to 255, ...) at most 64 rows name the same one
- gate_probs: bfloat16 [4096, 2], P(('rep', 'exp')), may hold values from 0.049804688 to 0.59765625
- w_gate: bfloat16 [8, 2048, 768], P('exp'), may hold values from -0.125 to 0.125
- w_up: bfloat16 [8, 2048, 768], P('exp'), may hold values from -0.125 to 0.125
- w_down: bfloat16 [8, 2048, 768], P('exp'), may hold values from -0.21875 to 0.21875
Outputs:
- in_grad: bfloat16 [4096, 2048], P(('rep', 'exp'))
- gate_grad: bfloat16 [4096, 2], P(('rep', 'exp'))
- delta_gate: bfloat16 [8, 2048, 768], P('exp', 'rep')
- delta_up: bfloat16 [8, 2048, 768], P('exp', 'rep')
- delta_down: bfloat16 [8, 2048, 768], P('exp', 'rep')
The draws below stay inside these ranges and needn't reach their ends.
Inputs may be any that keep to these rules, and one draw needn't show every extreme that they name: `expert_ids`: the 2 entries of a token name different experts. Among the 128 tokens of one device (aligned blocks in token order) no expert is named by more than 64 entries, and in every draw some expert is named by exactly 64 entries of some device. Every expert is named somewhere.
All inputs are finite; a program needn't handle non-finite values.
Results may differ from the reference program's by a relative error of at most 0.012.
Values may be sent and summed in bfloat16 or wider, within the bound.
No kernel may reach another device: no remote copies, remote signals or barrier semaphores. Data moves between devices by JAX's collectives and lax.ppermute only.
A program may use at most 128 MiB of HBM per device.

```python
import math
import jax
import jax.numpy as jnp
import numpy as np
from jax import lax

D = 2048
FF = 768
TOP = 2
TOK_DEV = 128
EXPERTS = 8
CAP = 64
TOKENS = 4096
N_REP = 4
N_EXP = 8


def block_levels(own_key, extent, cuts, least, top_value):
    def one(dim, parts):
        steps = jax.random.uniform(jax.random.fold_in(jax.random.fold_in(own_key, 6), dim), (parts,), jnp.float32, least / len(cuts), top_value / len(cuts))
        return jnp.repeat(jnp.exp(steps), extent[dim] // parts).reshape((-1,) + (1,) * (len(extent) - dim - 1))

    loudness = one(*cuts[0])
    for cut in cuts[1:]:
        loudness = loudness * one(*cut)
    return loudness


def assign_block(stream_key, own, number, rows, count, top, limit, slope):
    order = jax.random.permutation(stream_key, count)
    packed, ordinary = shares(count, rows * top, limit, slope, True), shares(count, rows * top, limit, slope, False)
    places = jnp.arange(count)

    def named(sizes, turn):
        used = int((sizes > 0).sum())
        fixed = max(1, used // 4)
        shifted = fixed + (places - fixed + turn * (used - fixed)) % max(1, count - fixed)
        return jnp.zeros((count,), jnp.int32).at[order[jnp.where(places < fixed, places, shifted)]].set(jnp.asarray(sizes, jnp.int32))

    sizes = jnp.where(number % 4 == 0, named(packed, number // 4), named(ordinary, number - number // 4 - 1))
    mixed = jax.random.permutation(jax.random.fold_in(own, 3), count)
    donor, sink = mixed[0:count // 2 * 2:2], mixed[1:count // 2 * 2:2]
    room = jnp.minimum(sizes[donor] - 1, limit - sizes[sink]) // 2
    room = jnp.where((donor == order[0]) | (sink == order[0]) | (sizes[sink] == 0), 0, jnp.maximum(room, 0))
    shifted = jax.random.randint(jax.random.fold_in(own, 4), (count // 2,), 0, 1 << 20) % (room + 1)
    sizes = sizes.at[donor].add(-shifted).at[sink].add(shifted)
    members = jnp.searchsorted(jnp.cumsum(sizes), jnp.arange(rows * top), side="right").astype(jnp.int32)
    grid = members.reshape(top, rows).T
    grid = grid[jax.random.permutation(jax.random.fold_in(own, 1), rows)]
    turn = jax.random.randint(jax.random.fold_in(own, 2), (rows, 1), 0, top)
    return jnp.take_along_axis(grid, (jnp.arange(top)[None, :] + turn) % top, axis=1)


def shares(count, total, bound, skew, full):
    loads = [(1 << 20) // math.isqrt(rank ** skew) + 1 for rank in range(1, count + 1)]
    largest = bound if full else min(bound, max(-(-total // count), total * loads[0] // sum(loads)))
    least = 1 if total - largest >= count - 1 else 0
    given, surplus = [largest] + [least] * (count - 1), total - largest - least * (count - 1)
    while surplus > 0:
        candidates = [i for i in range(1, count) if given[i] < largest] or [i for i in range(1, count) if given[i] < bound]
        pool, budget = sum([loads[i] for i in candidates]), surplus
        for i in candidates:
            addition = min(bound - given[i], max(1, budget * loads[i] // pool), surplus)
            given[i] = given[i] + addition
            surplus = surplus - addition
    return np.array(given)


def normal_values(stream_key, dims, spread, bound, pieces=(), kind=jnp.bfloat16):
    result = jax.random.normal(stream_key, dims, jnp.float32) * spread
    if len(pieces) > 0:
        result = block_levels(stream_key, dims, pieces, -0.22, 0.18) * result
    return jnp.clip(result, min=-bound, max=bound).astype(kind)


def setup_inputs(seed: int = 0) -> dict:
    key_of = jax.random.split(jax.random.key(seed), 8)
    features = normal_values(key_of[0], (TOKENS, D), 1.0, 6.0, ((0, 32),))
    out_grad = normal_values(key_of[1], (TOKENS, D), 0.25, 1.5, ((0, 32),))
    expert_ids_keys = jax.random.split(jax.random.fold_in(key_of[2], 1), TOKENS // TOK_DEV)
    expert_ids_turns = jax.random.permutation(jax.random.fold_in(key_of[2], 3), TOKENS // TOK_DEV)
    expert_ids = jax.vmap(lambda own, number: assign_block(jax.random.fold_in(key_of[2], 2), own, number, TOK_DEV, EXPERTS, TOP, CAP, 2))(expert_ids_keys, expert_ids_turns).reshape((TOKENS, TOP))
    gate_probs = jnp.clip(jnp.exp(math.log(0.59765625) - 2.4849066 * jax.random.uniform(key_of[3], (TOKENS, TOP), jnp.float32) ** block_levels(key_of[3], (TOKENS, TOP), ((0, 32),), -0.2, 0.2)), 0.049804688, 0.59765625).astype(jnp.bfloat16)
    w_gate = normal_values(key_of[4], (EXPERTS, D, FF), D ** -0.5, 0.125, ((0, 8),))
    w_up = normal_values(key_of[5], (EXPERTS, D, FF), D ** -0.5, 0.125, ((0, 8),))
    w_down = normal_values(key_of[6], (EXPERTS, D, FF), FF ** -0.5, 0.21875, ((0, 8),))
    return {"features": features, "out_grad": out_grad, "expert_ids": expert_ids, "gate_probs": gate_probs, "w_gate": w_gate, "w_up": w_up, "w_down": w_down}


def dot_rows(matrix_a, matrix_b):
    return lax.dot_general(matrix_a, matrix_b, (((0,), (0,)), ((), ())), preferred_element_type=jnp.float32)


def dot_last(matrix_a, matrix_b):
    return lax.dot_general(matrix_a, matrix_b, (((1,), (1,)), ((), ())), preferred_element_type=jnp.float32)


def expert_terms(inputs, gate_mat, up_mat, down_mat):
    rows_x, rows_dy, rows_g = inputs
    pre_gate = jnp.dot(rows_x, gate_mat, preferred_element_type=jnp.float32)
    pre_up = jnp.dot(rows_x, up_mat, preferred_element_type=jnp.float32)
    gate_sig = jax.nn.sigmoid(pre_gate)
    gate_act = pre_gate * gate_sig
    hidden = (gate_act * pre_up).astype(jnp.bfloat16)
    back_grad = jnp.dot(rows_dy, down_mat, preferred_element_type=jnp.float32)
    gate_row = jnp.sum(back_grad * hidden.astype(jnp.float32), axis=1).astype(jnp.bfloat16)
    scaled = (rows_g * rows_dy.astype(jnp.float32)).astype(jnp.bfloat16)
    d_hidden = rows_g * back_grad
    d_gate = (d_hidden * pre_up * gate_sig * (1.0 + pre_gate * (1.0 - gate_sig))).astype(jnp.bfloat16)
    d_up = (d_hidden * gate_act).astype(jnp.bfloat16)
    row_grad = (dot_last(d_gate, gate_mat) + dot_last(d_up, up_mat)).astype(jnp.bfloat16)
    return row_grad, gate_row, hidden, scaled, d_gate, d_up


def rounded(value):
    return lax.optimization_barrier(value.astype(jnp.bfloat16)).astype(jnp.float32)


def reference(features, out_grad, expert_ids, gate_probs, w_gate, w_up, w_down):
    block = N_EXP * TOK_DEV
    slot_total = N_EXP * CAP
    feats = features.reshape(N_REP, block, D)
    grads = out_grad.reshape(N_REP, block, D)
    gates = gate_probs.reshape(N_REP, block, TOP)
    routes = expert_ids.reshape(N_REP, block * TOP)
    entries = jnp.arange(block * TOP, dtype=jnp.int32)

    def per_expert(carry, expert):
        in_acc, gate_acc = carry
        sum_gate = jnp.zeros((D, FF), jnp.float32)
        sum_up = jnp.zeros((D, FF), jnp.float32)
        sum_down = jnp.zeros((D, FF), jnp.float32)
        for replica in range(N_REP):
            chosen = routes[replica] == expert
            position = jnp.cumsum(chosen.astype(jnp.int32)) - 1
            target = jnp.where(chosen, position, slot_total).astype(jnp.int32)
            picked = jnp.zeros((slot_total + 1,), jnp.int32).at[target].set(entries)[:slot_total]
            valid = jnp.zeros((slot_total + 1,), jnp.float32).at[target].set(1.0)[:slot_total]
            token_idx = (picked // TOP).astype(jnp.int32)
            rank_idx = (picked % TOP).astype(jnp.int32)
            keep = valid.astype(jnp.bfloat16)[:, None]
            rows_x = feats[replica][token_idx] * keep
            rows_dy = grads[replica][token_idx] * keep
            rows_g = (gates[replica][token_idx, rank_idx].astype(jnp.float32) * valid)[:, None]
            row_grad, gate_row, hidden, scaled, d_gate, d_up = expert_terms(
                (rows_x, rows_dy, rows_g), w_gate[expert], w_up[expert], w_down[expert])
            in_acc = in_acc.at[replica, token_idx].add(row_grad.astype(jnp.float32) * valid[:, None])
            gate_acc = gate_acc.at[replica, token_idx, rank_idx].add(gate_row.astype(jnp.float32) * valid)
            sum_gate = sum_gate + rounded(dot_rows(rows_x, d_gate))
            sum_up = sum_up + rounded(dot_rows(rows_x, d_up))
            sum_down = sum_down + rounded(dot_rows(scaled, hidden))
        deltas = ((sum_gate / N_REP).astype(jnp.bfloat16), (sum_up / N_REP).astype(jnp.bfloat16),
                  (sum_down / N_REP).astype(jnp.bfloat16))
        return (in_acc, gate_acc), deltas

    start = (jnp.zeros((N_REP, block, D), jnp.float32), jnp.zeros((N_REP, block, TOP), jnp.float32))
    (in_acc, gate_acc), stacked = lax.scan(per_expert, start, jnp.arange(EXPERTS, dtype=jnp.int32))
    in_grad = in_acc.reshape(TOKENS, D).astype(jnp.bfloat16)
    gate_grad = gate_acc.reshape(TOKENS, TOP).astype(jnp.bfloat16)
    return in_grad, gate_grad, stacked[0], stacked[1], stacked[2]
```

```python
import jax
import jax.numpy as jnp
from jax import lax
from jax.sharding import PartitionSpec as P

F32 = jnp.float32
BF16 = jnp.bfloat16


def dot_rows(matrix_a, matrix_b):
    return lax.dot_general(
        matrix_a, matrix_b, (((0,), (0,)), ((), ())), preferred_element_type=F32
    )


def dot_last(matrix_a, matrix_b):
    return lax.dot_general(
        matrix_a, matrix_b, (((1,), (1,)), ((), ())), preferred_element_type=F32
    )


def route(meta, tokens, top_k, capacity):
    senders = meta.shape[0] // tokens
    me = lax.axis_index("exp")
    ids = meta[:, :top_k].reshape(senders, tokens, top_k)
    probs = meta[:, top_k:].reshape(senders, tokens, top_k)
    hit = ids == me.astype(BF16)
    named = jnp.any(hit, axis=2)
    gate = jnp.sum(jnp.where(hit, probs, 0).astype(F32), axis=2)
    upto = (jnp.arange(tokens)[:, None] <= jnp.arange(tokens)[None, :]).astype(BF16)
    rank = jnp.dot(named.astype(BF16), upto, preferred_element_type=F32) - 1.0
    slots = jnp.arange(capacity, dtype=F32)
    chosen = named[:, None, :] & (rank[:, None, :] == slots[None, :, None])
    rows_g = jnp.sum(jnp.where(chosen, gate[:, None, :], 0.0), axis=2)
    return hit, chosen, rows_g.reshape(senders * capacity, 1)


def pick(select, dense):
    senders, capacity, tokens = select.shape
    rows = lax.dot_general(
        select,
        dense.reshape(senders, tokens, -1),
        (((2,), (1,)), ((0,), (0,))),
        preferred_element_type=F32,
    )
    return rows.astype(BF16).reshape(senders * capacity, -1)


def spread(select, rows):
    senders, capacity, tokens = select.shape
    dense = lax.dot_general(
        select,
        rows.reshape(senders, capacity, -1),
        (((1,), (1,)), ((0,), (0,))),
        preferred_element_type=F32,
    )
    return dense.astype(BF16).reshape(senders * tokens, -1)


def on_device(features, out_grad, expert_ids, gate_probs, w_gate, w_up, w_down):
    tokens, model_width = features.shape
    top_k = expert_ids.shape[1]
    experts = lax.axis_size("exp")
    replicas = lax.axis_size("rep")
    capacity = min(tokens, 2 * tokens * top_k // experts)
    gate_mat, up_mat, down_mat = (w_gate[0], w_up[0], w_down[0])

    meta = jnp.concatenate([expert_ids.astype(BF16), gate_probs], axis=1)
    meta = lax.all_gather(meta, "exp", axis=0, tiled=True)
    all_x = lax.all_gather(features, "exp", axis=0, tiled=True)
    all_dy = lax.all_gather(out_grad, "exp", axis=0, tiled=True)

    hit, chosen, rows_g = route(meta, tokens, top_k, capacity)
    select = chosen.astype(BF16)
    rows_x = pick(select, all_x)
    pre_gate = jnp.dot(rows_x, gate_mat, preferred_element_type=F32)
    pre_up = jnp.dot(rows_x, up_mat, preferred_element_type=F32)
    gate_sig = jax.nn.sigmoid(pre_gate)
    gate_act = pre_gate * gate_sig
    hidden = (gate_act * pre_up).astype(BF16)

    rows_dy = pick(select, all_dy)
    back_grad = jnp.dot(rows_dy, down_mat, preferred_element_type=F32)
    gate_row = jnp.sum(back_grad * hidden.astype(F32), axis=1).astype(BF16)
    scaled = (rows_g * rows_dy.astype(F32)).astype(BF16)
    d_hidden = rows_g * back_grad
    d_gate = (d_hidden * pre_up * gate_sig * (1.0 + pre_gate * (1.0 - gate_sig))).astype(BF16)
    d_up = (d_hidden * gate_act).astype(BF16)

    def delta(left, right):
        part = dot_rows(left, right).astype(BF16)
        total = lax.psum_scatter(part, "rep", scatter_dimension=0, tiled=True)
        return (total.astype(F32) / replicas).astype(BF16)[None]

    delta_down = delta(scaled, hidden)
    delta_gate = delta(rows_x, d_gate)
    delta_up = delta(rows_x, d_up)

    row_grad = (dot_last(d_gate, gate_mat) + dot_last(d_up, up_mat)).astype(BF16)
    in_grad = lax.psum_scatter(
        spread(select, row_grad), "exp", scatter_dimension=0, tiled=True
    )
    gate_dense = jnp.sum(
        jnp.where(chosen, gate_row.astype(F32).reshape(experts, capacity, 1), 0.0), axis=1
    )
    gate_dense = jnp.where(hit, gate_dense[:, :, None], 0.0).astype(BF16)
    gate_grad = lax.psum_scatter(
        gate_dense.reshape(experts * tokens, top_k), "exp", scatter_dimension=0, tiled=True
    )
    return (in_grad, gate_grad, delta_gate, delta_up, delta_down)


def solution(mesh):
    by_token = P(("rep", "exp"), None)
    by_expert = P("exp", None, None)
    by_shard = P("exp", "rep", None)
    return jax.shard_map(
        on_device,
        mesh=mesh,
        in_specs=(by_token,) * 4 + (by_expert,) * 3,
        out_specs=(by_token,) * 2 + (by_shard,) * 3,
        check_vma=False,
    )
```

```python
import jax
import jax.numpy as jnp
from jax import lax
from jax.sharding import PartitionSpec as P

F32 = jnp.float32
BF16 = jnp.bfloat16
CORES = 2


def dot_rows(matrix_a, matrix_b):
    return lax.dot_general(
        matrix_a, matrix_b, (((0,), (0,)), ((), ())), preferred_element_type=F32
    )


def dot_last(matrix_a, matrix_b):
    return lax.dot_general(
        matrix_a, matrix_b, (((1,), (1,)), ((), ())), preferred_element_type=F32
    )


def dot_plain(matrix_a, matrix_b):
    return jnp.dot(matrix_a, matrix_b, preferred_element_type=F32)


def to_chip(value, experts, hop, flip):
    chips = experts // CORES
    pairs = [
        (chip * CORES + core, (chip + hop) % chips * CORES + (core ^ flip))
        for chip in range(chips)
        for core in range(CORES)
    ]
    return lax.ppermute(value, "exp", pairs)


def route(meta, top_k, capacity):
    tokens = meta.shape[1]
    hit = meta[:top_k] == lax.axis_index("exp").astype(BF16)
    named = jnp.any(hit, axis=0, keepdims=True)
    gate = jnp.sum(jnp.where(hit, meta[top_k:], 0).astype(F32), axis=0, keepdims=True)
    upto = (jnp.arange(tokens)[:, None] <= jnp.arange(tokens)[None, :]).astype(BF16)
    rank = dot_plain(named.astype(BF16), upto) - 1.0
    chosen = named & (rank == jnp.arange(capacity, dtype=F32)[:, None])
    return hit, chosen, jnp.sum(jnp.where(chosen, gate, 0.0), axis=1, keepdims=True)


def swap_reduce(parts, bits):
    replicas = lax.axis_size("rep")
    held = dict(parts)
    for bit in bits:
        leaving = [i for i in held if i & bit]
        pairs = [(r, r ^ bit) for r in range(replicas)]
        sent = jnp.concatenate([held[i] for i in leaving], axis=0)
        came = lax.ppermute(sent, "rep", pairs)
        rows = held[leaving[0]].shape[0]
        total = {}
        for place, i in enumerate(leaving):
            keep = i ^ bit
            total[keep] = held[keep].astype(F32) + came[place * rows : (place + 1) * rows].astype(F32)
        held = total if len(total) == 1 else {i: v.astype(BF16) for i, v in total.items()}
    return held[0]


def on_device(features, out_grad, expert_ids, gate_probs, w_gate, w_up, w_down):
    tokens, model_width = features.shape
    top_k = expert_ids.shape[1]
    hidden_units = w_gate.shape[2]
    experts = lax.axis_size("exp")
    replicas = lax.axis_size("rep")
    chips = experts // CORES
    capacity = min(tokens, 2 * tokens * top_k // experts)
    gate_mat, up_mat, down_mat = (w_gate[0], w_up[0], w_down[0])
    sources = [(hop, flip) for hop in range(chips) for flip in range(CORES)]

    meta = jnp.concatenate([expert_ids.T.astype(BF16), gate_probs.T], axis=0)
    routes = {}
    for hop, flip in sources:
        block = meta if hop + flip == 0 else to_chip(meta, experts, hop, flip)
        routes[hop, flip] = route(block, top_k, capacity)

    rows_x, rows_dy = [], []
    block_x, block_dy = features, out_grad
    for hop in range(chips):
        for block, rows in ((block_x, rows_x), (block_dy, rows_dy)):
            for flip, one in ((0, block), (1, to_chip(block, experts, 0, 1))):
                select = routes[hop, flip][1].astype(BF16)
                rows.append(dot_plain(select, one).astype(BF16))
        if hop + 1 < chips:
            block_x = to_chip(block_x, experts, 1, 0)
            block_dy = to_chip(block_dy, experts, 1, 0)

    made = []
    for hop in range(chips):
        both = slice(hop * CORES, (hop + 1) * CORES)
        x = jnp.concatenate(rows_x[both], axis=0)
        dy = jnp.concatenate(rows_dy[both], axis=0)
        rows_g = jnp.concatenate([routes[source][2] for source in sources[both]], axis=0)
        pre_gate = dot_plain(x, gate_mat)
        pre_up = dot_plain(x, up_mat)
        gate_sig = jax.nn.sigmoid(pre_gate)
        gate_act = pre_gate * gate_sig
        hidden = (gate_act * pre_up).astype(BF16)
        back_grad = dot_plain(dy, down_mat)
        gate_row = jnp.sum(back_grad * hidden.astype(F32), axis=1, keepdims=True).astype(BF16)
        scaled = (rows_g * dy.astype(F32)).astype(BF16)
        d_hidden = rows_g * back_grad
        d_gate = d_hidden * pre_up * gate_sig * (1.0 + pre_gate * (1.0 - gate_sig))
        d_up = d_hidden * gate_act
        made.append((x, scaled, hidden, d_gate.astype(BF16), d_up.astype(BF16), gate_row))
    x, scaled, hidden, d_gate, d_up, gate_row = (jnp.concatenate(a, axis=0) for a in zip(*made))

    shard = model_width // replicas
    own = lax.axis_index("rep")
    bits = [1 << i for i in range(replicas.bit_length() - 1)]
    half = hidden_units // 2
    deltas = []
    for left, right in ((scaled, hidden), (x, d_gate), (x, d_up)):
        halves = []
        for columns, order in ((slice(0, half), bits), (slice(half, None), bits[::-1])):
            parts = {}
            for i in reversed(range(replicas)):
                chunk = lax.dynamic_slice_in_dim(left, (own ^ i) * shard, shard, axis=1)
                parts[i] = dot_rows(chunk, right[:, columns]).astype(BF16)
            halves.append(swap_reduce(parts, order))
        total = jnp.concatenate(halves, axis=1)
        deltas.append((total / replicas).astype(BF16)[None])
    delta_down, delta_gate, delta_up = deltas

    row_grad = (dot_last(d_gate, gate_mat) + dot_last(d_up, up_mat)).astype(BF16)
    dense, gates = {}, {}
    for place, source in enumerate(sources):
        hit, chosen, _ = routes[source]
        mine = slice(place * capacity, (place + 1) * capacity)
        dense[source] = dot_rows(chosen.astype(BF16), row_grad[mine]).astype(BF16)
        value = jnp.sum(jnp.where(chosen, gate_row[mine].astype(F32), 0.0), axis=0, keepdims=True)
        gates[source] = jnp.where(hit, value, 0.0).astype(BF16)

    def plus(a, b):
        return (a.astype(F32) + b.astype(F32)).astype(BF16)

    summed = {
        hop: plus(dense[hop, 0], to_chip(dense[hop, 1], experts, 0, 1)) for hop in range(chips)
    }
    in_grad = summed[1 % chips]
    for hop in range(2, chips + 1):
        in_grad = plus(to_chip(in_grad, experts, 1, 0), summed[hop % chips])
    gate_grad = gates[0, 0].astype(F32)
    for hop, flip in sources[1:]:
        gate_grad = gate_grad + to_chip(gates[hop, flip], experts, -hop, flip).astype(F32)
    return (in_grad, gate_grad.astype(BF16).T, delta_gate, delta_up, delta_down)


def solution(mesh):
    by_token = P(("rep", "exp"), None)
    by_expert = P("exp", None, None)
    by_shard = P("exp", "rep", None)
    return jax.shard_map(
        on_device,
        mesh=mesh,
        in_specs=(by_token,) * 4 + (by_expert,) * 3,
        out_specs=(by_token,) * 2 + (by_shard,) * 3,
        check_vma=False,
    )
```

```python
import jax
import jax.numpy as jnp
from jax import lax
from jax.sharding import PartitionSpec as P

F32 = jnp.float32
BF16 = jnp.bfloat16
CORES = 2
EXTRA = 8


def dot_rows(matrix_a, matrix_b):
    return lax.dot_general(
        matrix_a, matrix_b, (((0,), (0,)), ((), ())), preferred_element_type=F32
    )


def dot_last(matrix_a, matrix_b):
    return lax.dot_general(
        matrix_a, matrix_b, (((1,), (1,)), ((), ())), preferred_element_type=F32
    )


def dot_plain(matrix_a, matrix_b):
    return jnp.dot(matrix_a, matrix_b, preferred_element_type=F32)


def to_chip(value, experts, hop, flip):
    chips = experts // CORES
    pairs = [
        (chip * CORES + core, (chip + hop) % chips * CORES + (core ^ flip))
        for chip in range(chips)
        for core in range(CORES)
    ]
    return lax.ppermute(value, "exp", pairs)


def route(meta, top_k, capacity):
    tokens = meta.shape[1]
    hit = meta[:top_k] == lax.axis_index("exp").astype(BF16)
    named = jnp.any(hit, axis=0, keepdims=True)
    gate = jnp.sum(jnp.where(hit, meta[top_k:], 0).astype(F32), axis=0, keepdims=True)
    upto = (jnp.arange(tokens)[:, None] <= jnp.arange(tokens)[None, :]).astype(BF16)
    rank = dot_plain(named.astype(BF16), upto) - 1.0
    chosen = named & (rank == jnp.arange(capacity, dtype=F32)[:, None])
    return hit, chosen, jnp.sum(jnp.where(chosen, gate, 0.0), axis=1, keepdims=True)


def swap(value, bit):
    pairs = [(r, r ^ bit) for r in range(lax.axis_size("rep"))]
    return lax.ppermute(value, "rep", pairs)


def added(kept, came, kept_order, came_order, bit):
    rows = kept[0].shape[0]
    total = {}
    for mine, i in zip(kept, kept_order):
        other = came_order.index(i ^ bit)
        total[i] = mine + came[other * rows : (other + 1) * rows].astype(F32)
    return total


def finish(total, bits):
    for bit in bits:
        gone = [i for i in total if i & bit]
        kept = [i for i in total if not i & bit]
        came = swap(jnp.concatenate([total[i].astype(BF16) for i in gone], axis=0), bit)
        total = added([total[i] for i in kept], came, kept, gone, bit)
    return total[0]


def on_device(features, out_grad, expert_ids, gate_probs, w_gate, w_up, w_down):
    tokens, model_width = features.shape
    top_k = expert_ids.shape[1]
    hidden_units = w_gate.shape[2]
    experts = lax.axis_size("exp")
    replicas = lax.axis_size("rep")
    chips = experts // CORES
    capacity = min(tokens, 2 * tokens * top_k // experts)
    gate_mat, up_mat, down_mat = (w_gate[0], w_up[0], w_down[0])
    sources = [(hop, flip) for hop in range(chips) for flip in range(CORES)]

    meta = jnp.concatenate([expert_ids.T.astype(BF16), gate_probs.T], axis=0)
    meta = jnp.pad(meta, ((0, EXTRA - 2 * top_k), (0, model_width - tokens)))

    routes, arrived = {}, []
    block_x, block_dy = jnp.concatenate([features, meta], axis=0), out_grad
    for hop in range(chips):
        pair_x = (block_x, to_chip(block_x, experts, 0, 1))
        pair_dy = (block_dy, to_chip(block_dy, experts, 0, 1))
        arrived.append((pair_x, pair_dy))
        if hop + 1 < chips:
            block_dy = to_chip(block_dy, experts, 1, 0)
            block_x = to_chip(block_x, experts, 1, 0)

    dense = {}
    shard = model_width // replicas
    own = lax.axis_index("rep")
    bits = [1 << i for i in range(replicas.bit_length() - 1)]
    low, high = bits[0], bits[-1]
    order = [i for a, b in ((0, 0), (0, 1), (1, 1), (1, 0)) for i in range(replicas)
             if bool(i & low) == a and bool(i & high) == b]

    def by_shard(rows):
        cut = [lax.dynamic_slice_in_dim(rows, (own ^ i) * shard, shard, axis=1) for i in order]
        return jnp.concatenate(cut, axis=1)

    def expert_rows(hops):
        rows_x, rows_dy, rows_g = [], [], []
        for hop, flip in ((hop, flip) for hop in hops for flip in range(CORES)):
            block_x, block_dy = arrived[hop][0][flip], arrived[hop][1][flip]
            named = block_x[tokens : tokens + 2 * top_k, :tokens]
            routes[hop, flip] = route(named, top_k, capacity)
            select = routes[hop, flip][1].astype(BF16)
            rows_x.append(dot_plain(select, block_x[:tokens]).astype(BF16))
            rows_dy.append(dot_plain(select, block_dy).astype(BF16))
            rows_g.append(routes[hop, flip][2])
        x, dy, rows_g = (jnp.concatenate(a, axis=0) for a in (rows_x, rows_dy, rows_g))
        pre_gate = dot_plain(x, gate_mat)
        pre_up = dot_plain(x, up_mat)
        gate_sig = jax.nn.sigmoid(pre_gate)
        gate_act = pre_gate * gate_sig
        hidden = (gate_act * pre_up).astype(BF16)
        back_grad = dot_plain(dy, down_mat)
        gate_row = jnp.sum(back_grad * hidden.astype(F32), axis=1, keepdims=True).astype(BF16)
        scaled = (rows_g * dy.astype(F32)).astype(BF16)
        d_hidden = rows_g * back_grad
        d_gate = d_hidden * pre_up * gate_sig * (1.0 + pre_gate * (1.0 - gate_sig))
        d_up = d_hidden * gate_act
        return (x, scaled, hidden, d_gate.astype(BF16), d_up.astype(BF16), gate_row)

    def sent_back(hops, d_gate, d_up, gate_row):
        row_grad = (dot_last(d_gate, gate_mat) + dot_last(d_up, up_mat)).astype(BF16)
        for place, source in enumerate((hop, flip) for hop in hops for flip in range(CORES)):
            hit, chosen, _ = routes[source]
            mine = slice(place * capacity, (place + 1) * capacity)
            rows = dot_rows(chosen.astype(BF16), row_grad[mine]).astype(BF16)
            value = jnp.where(chosen, gate_row[mine].astype(F32), 0.0)
            gates = jnp.where(hit, jnp.sum(value, axis=0, keepdims=True), 0.0).astype(BF16)
            gates = jnp.pad(gates, ((0, EXTRA - top_k), (0, model_width - tokens)))
            dense[source] = jnp.concatenate([rows, gates], axis=0)

    half = hidden_units // 2
    ways = ((slice(0, half), bits), (slice(half, None), bits[::-1]))

    def sorted_by(way, gone):
        return [i for i in order if bool(i & way[1][0]) == gone]

    def products(left, right, gone):
        made = []
        for way in ways:
            columns = right[:, way[0]]
            start = order.index(sorted_by(way, gone)[0]) * shard
            if gone:
                made.append(dot_rows(left[:, start : start + model_width // 2], columns))
            else:
                cut = [order.index(i) * shard for i in sorted_by(way, gone)]
                made.append([dot_rows(left[:, at : at + shard], columns) for at in cut])
        return made

    early, late = range(chips - 1), range(chips - 1, chips)
    x, scaled, hidden, d_gate, d_up, gate_row = (
        jnp.concatenate(a, axis=0) for a in zip(*[expert_rows([hop]) for hop in early])
    )
    sent_back(early, d_gate, d_up, gate_row)
    pairs = ((by_shard(scaled), hidden), (by_shard(x), d_gate), (by_shard(x), d_up))
    gone_early = [products(left, right, True) for left, right in pairs]
    stay_early = [products(left, right, False) for left, right in pairs]

    gone_early, dense, arrived[-1] = lax.optimization_barrier((gone_early, dense, arrived[-1]))
    x, scaled, hidden, d_gate, d_up, gate_row = expert_rows(late)
    pairs = [[by_shard(scaled), hidden], [by_shard(x), d_gate], [by_shard(x), d_up]]

    def leaves(m):
        both = zip(gone_early[m], products(*pairs[m], True), ways)
        return [(before + after).astype(BF16) for before, after, _ in both]

    gone = leaves(0)
    gone, pairs[1:] = lax.optimization_barrier((gone, pairs[1:]))
    came = [[swap(value, way[1][0]) for value, way in zip(gone, ways)]]
    gone = leaves(1)
    gone, pairs[2] = lax.optimization_barrier((gone, pairs[2]))
    came.append([swap(value, way[1][0]) for value, way in zip(gone, ways)])
    gone = leaves(2)
    came[0], gone, pairs, d_gate, d_up = lax.optimization_barrier((came[0], gone, pairs, d_gate, d_up))
    came.append([swap(value, way[1][0]) for value, way in zip(gone, ways)])
    sent_back(late, d_gate, d_up, gate_row)

    def delta(m):
        halves = []
        stays = zip(ways, came[m], stay_early[m], products(*pairs[m], False))
        for way, value, before, after in stays:
            kept = [(a + b).astype(BF16).astype(F32) for a, b in zip(before, after)]
            total = added(kept, value, sorted_by(way, False), sorted_by(way, True), way[1][0])
            halves.append(finish(total, way[1][1:]))
        return (jnp.concatenate(halves, axis=1) / replicas).astype(BF16)[None]

    delta_down, delta_gate, delta_up = delta(0), delta(1), delta(2)

    def plus(a, b):
        return (a.astype(F32) + b.astype(F32)).astype(BF16)

    summed = {
        hop: plus(dense[hop, 0], to_chip(dense[hop, 1], experts, 0, 1)) for hop in range(chips)
    }
    in_grad = summed[1 % chips]
    for hop in range(2, chips + 1):
        in_grad = plus(to_chip(in_grad, experts, 1, 0), summed[hop % chips])
    gate_grad = in_grad[tokens : tokens + top_k, :tokens].T
    return (in_grad[:tokens], gate_grad, delta_gate, delta_up, delta_down)


def solution(mesh):
    by_token = P(("rep", "exp"), None)
    by_expert = P("exp", None, None)
    by_shard = P("exp", "rep", None)
    return jax.shard_map(
        on_device,
        mesh=mesh,
        in_specs=(by_token,) * 4 + (by_expert,) * 3,
        out_specs=(by_token,) * 2 + (by_shard,) * 3,
        check_vma=False,
    )
```

```python
import jax
import jax.numpy as jnp
from jax import lax
from jax.sharding import PartitionSpec as P

F32 = jnp.float32
BF16 = jnp.bfloat16
CORES = 2
EXTRA = 8


def dot_rows(matrix_a, matrix_b):
    return lax.dot_general(
        matrix_a, matrix_b, (((0,), (0,)), ((), ())), preferred_element_type=F32
    )


def dot_last(matrix_a, matrix_b):
    return lax.dot_general(
        matrix_a, matrix_b, (((1,), (1,)), ((), ())), preferred_element_type=F32
    )


def dot_plain(matrix_a, matrix_b):
    return jnp.dot(matrix_a, matrix_b, preferred_element_type=F32)


def to_chip(value, experts, hop, flip):
    chips = experts // CORES
    pairs = [
        (chip * CORES + core, (chip + hop) % chips * CORES + (core ^ flip))
        for chip in range(chips)
        for core in range(CORES)
    ]
    return lax.ppermute(value, "exp", pairs)


def route(meta, top_k, capacity):
    tokens = meta.shape[1]
    hit = meta[:top_k] == lax.axis_index("exp").astype(BF16)
    named = jnp.any(hit, axis=0, keepdims=True)
    gate = jnp.sum(jnp.where(hit, meta[top_k:], 0).astype(F32), axis=0, keepdims=True)
    upto = (jnp.arange(tokens)[:, None] <= jnp.arange(tokens)[None, :]).astype(BF16)
    rank = dot_plain(named.astype(BF16), upto) - 1.0
    chosen = named & (rank == jnp.arange(capacity, dtype=F32)[:, None])
    return hit, chosen, jnp.sum(jnp.where(chosen, gate, 0.0), axis=1, keepdims=True)


def to_replica(value, bit_of_core):
    experts = lax.axis_size("exp")
    pairs = [
        (r * experts + e, (r ^ bit_of_core[e % CORES]) * experts + e)
        for r in range(lax.axis_size("rep"))
        for e in range(experts)
    ]
    return lax.ppermute(value, ("rep", "exp"), pairs)


def on_device(features, out_grad, expert_ids, gate_probs, w_gate, w_up, w_down):
    tokens, model_width = features.shape
    top_k = expert_ids.shape[1]
    hidden_units = w_gate.shape[2]
    experts = lax.axis_size("exp")
    replicas = lax.axis_size("rep")
    chips = experts // CORES
    capacity = min(tokens, 2 * tokens * top_k // experts)
    gate_mat, up_mat, down_mat = (w_gate[0], w_up[0], w_down[0])

    meta = jnp.concatenate([expert_ids.T.astype(BF16), gate_probs.T], axis=0)
    meta = jnp.pad(meta, ((0, EXTRA - 2 * top_k), (0, model_width - tokens)))

    bits = [1 << i for i in range(replicas.bit_length() - 1)]
    turns = list(zip(bits, bits[::-1]))
    own, core = lax.axis_index("rep"), lax.axis_index("exp") % CORES
    shard, half = model_width // replicas, hidden_units // 2
    upper = (own & jnp.where(core == 0, *turns[0])) != 0

    def my_half(value):
        return lax.dynamic_slice_in_dim(value, jnp.where(upper, half, 0), half, axis=1)

    def by_shard(rows):
        cut = []
        for i in range(replicas):
            masks = [sum(turn[c] for j, turn in enumerate(turns) if i >> j & 1) for c in range(CORES)]
            at = (own ^ jnp.where(core == 0, *masks)) * shard
            cut.append(lax.dynamic_slice_in_dim(rows, at, shard, axis=1))
        return jnp.concatenate(cut, axis=1)

    def expert_rows(x, dy, rows_g, weights):
        pre_gate = dot_plain(x, weights[0])
        pre_up = dot_plain(x, weights[1])
        gate_sig = jax.nn.sigmoid(pre_gate)
        gate_act = pre_gate * gate_sig
        hidden = (gate_act * pre_up).astype(BF16)
        back_grad = dot_plain(dy, weights[2])
        scaled = (rows_g * dy.astype(F32)).astype(BF16)
        d_hidden = rows_g * back_grad
        d_gate = d_hidden * pre_up * gate_sig * (1.0 + pre_gate * (1.0 - gate_sig))
        d_up = d_hidden * gate_act
        gate_row = jnp.sum(back_grad * hidden.astype(F32), axis=1, keepdims=True).astype(BF16)
        return scaled, hidden, d_gate.astype(BF16), d_up.astype(BF16), gate_row

    routes, dense = {}, {}

    def at_home(hop, pair_x, pair_dy):
        rows_x, rows_dy, rows_g = [], [], []
        for flip in range(CORES):
            named = pair_x[flip][tokens : tokens + 2 * top_k, :tokens]
            routes[hop, flip] = route(named, top_k, capacity)
            select = routes[hop, flip][1].astype(BF16)
            rows_x.append(dot_plain(select, pair_x[flip][:tokens]).astype(BF16))
            rows_dy.append(dot_plain(select, pair_dy[flip]).astype(BF16))
            rows_g.append(routes[hop, flip][2])
        x, dy, rows_g = (jnp.concatenate(a, axis=0) for a in (rows_x, rows_dy, rows_g))
        gates = jnp.pad(rows_g.astype(BF16).T, ((0, EXTRA - 1), (0, model_width - rows_g.shape[0])))
        shared = (to_replica(jnp.concatenate([dy, gates], axis=0), turns[0]), to_replica(x, turns[0]))
        scaled, hidden, d_gate, d_up, gate_row = expert_rows(x, dy, rows_g, (gate_mat, up_mat, down_mat))
        terms = (scaled, x, my_half(hidden), my_half(d_gate), my_half(d_up))
        return terms, shared, (d_gate, d_up, gate_row)

    def of_partner(shared):
        block, x = shared
        rows = x.shape[0]
        rows_g = block[rows : rows + 1, :rows].T.astype(F32)
        scaled, hidden, d_gate, d_up, _ = expert_rows(x, block[:rows], rows_g, half_mats)
        return scaled, x, hidden, d_gate, d_up

    def sent_back(hops, d_gate, d_up, gate_row):
        row_grad = (dot_last(d_gate, gate_mat) + dot_last(d_up, up_mat)).astype(BF16)
        for place, source in enumerate((hop, flip) for hop in hops for flip in range(CORES)):
            hit, chosen, _ = routes[source]
            mine = slice(place * capacity, (place + 1) * capacity)
            rows = dot_rows(chosen.astype(BF16), row_grad[mine]).astype(BF16)
            value = jnp.where(chosen, gate_row[mine].astype(F32), 0.0)
            gates = jnp.where(hit, jnp.sum(value, axis=0, keepdims=True), 0.0).astype(BF16)
            gates = jnp.pad(gates, ((0, EXTRA - top_k), (0, model_width - tokens)))
            dense[source] = jnp.concatenate([rows, gates], axis=0)

    def joined(groups):
        return [jnp.concatenate(a, axis=0) for a in zip(*groups)]

    kept = max(replicas // 2, CORES) * shard

    def products(terms):
        scaled, x, hidden, d_gate, d_up = terms
        scaled, x = by_shard(scaled), by_shard(x)
        pairs = ((scaled, hidden), (x, d_gate), (x, d_up))
        gone = [dot_rows(left[:, kept:], right) for left, right in pairs]
        return gone, [dot_rows(left[:, :kept], right) for left, right in pairs]

    half_mats = [my_half(value) for value in (gate_mat, up_mat, down_mat)]
    block_x, block_dy = jnp.concatenate([features, meta], axis=0), out_grad
    home, partner, back = [], [], []
    for hop in range(chips):
        pair_x = (block_x, to_chip(block_x, experts, 0, 1))
        pair_dy = (block_dy, to_chip(block_dy, experts, 0, 1))
        if hop + 1 < chips:
            block_dy = to_chip(block_dy, experts, 1, 0)
            block_x = to_chip(block_x, experts, 1, 0)
        else:
            sent_back(range(hop), *joined(back))
            gone_early, stay_early = products(joined(home + [of_partner(p) for p in partner[:-1]]))
            gone_early, dense, pair_x, pair_dy = lax.optimization_barrier(
                (gone_early, dense, pair_x, pair_dy)
            )
            partner = partner[-1:]
            home, back = [], []
        terms, shared, grads = at_home(hop, pair_x, pair_dy)
        home.append(terms)
        partner.append(shared)
        back.append(grads)

    gone, stay = products(joined(home + [of_partner(p) for p in partner]))
    gone = [(before + after).astype(BF16) for before, after in zip(gone_early, gone)]
    stay = [before + after for before, after in zip(stay_early, stay)]
    deltas = []
    for m in range(3):
        total = stay[m]
        for turn in turns[:0:-1]:
            size = total.shape[0]
            if turn is not turns[-1]:
                size = size // 2
                gone[m], total = total[size:].astype(BF16), total[:size]
            total = total + to_replica(gone[m], turn).astype(F32)
        total = (total / replicas).astype(BF16)
        mine, came = total[:shard], to_replica(total[shard:], turns[0])
        lower_columns = jnp.where(upper, came, mine)
        upper_columns = jnp.where(upper, mine, came)
        deltas.append(jnp.concatenate([lower_columns, upper_columns], axis=1)[None])
    delta_down, delta_gate, delta_up = deltas
    sent_back([chips - 1], *back[0])

    def plus(a, b):
        return (a.astype(F32) + b.astype(F32)).astype(BF16)

    def other_core(hops):
        swapped = to_chip(jnp.concatenate([dense[hop, 1] for hop in hops], axis=0), experts, 0, 1)
        rows = tokens + EXTRA
        return [swapped[i * rows : (i + 1) * rows] for i in range(len(hops))]

    swapped = other_core(range(chips - 1)) + other_core([chips - 1])
    summed = [plus(dense[hop, 0], swapped[hop]) for hop in range(chips)]
    in_grad = summed[1 % chips]
    for hop in range(2, chips + 1):
        in_grad = plus(to_chip(in_grad, experts, 1, 0), summed[hop % chips])
    gate_grad = in_grad[tokens : tokens + top_k, :tokens].T
    return (in_grad[:tokens], gate_grad, delta_gate, delta_up, delta_down)


def solution(mesh):
    by_token = P(("rep", "exp"), None)
    by_expert = P("exp", None, None)
    by_shard = P("exp", "rep", None)
    return jax.shard_map(
        on_device,
        mesh=mesh,
        in_specs=(by_token,) * 4 + (by_expert,) * 3,
        out_specs=(by_token,) * 2 + (by_shard,) * 3,
        check_vma=False,
    )
```

```python
import jax
import jax.numpy as jnp
from jax import lax
from jax.sharding import PartitionSpec as P

F32 = jnp.float32
BF16 = jnp.bfloat16
CORES = 2
EXTRA = 8


def dot_rows(matrix_a, matrix_b):
    return lax.dot_general(
        matrix_a, matrix_b, (((0,), (0,)), ((), ())), preferred_element_type=F32
    )


def dot_last(matrix_a, matrix_b):
    return lax.dot_general(
        matrix_a, matrix_b, (((1,), (1,)), ((), ())), preferred_element_type=F32
    )


def dot_plain(matrix_a, matrix_b):
    return jnp.dot(matrix_a, matrix_b, preferred_element_type=F32)


def to_chip(value, experts, hop, flip):
    chips = experts // CORES
    pairs = [
        (chip * CORES + core, (chip + hop) % chips * CORES + (core ^ flip))
        for chip in range(chips)
        for core in range(CORES)
    ]
    return lax.ppermute(value, "exp", pairs)


def route(meta, top_k, capacity):
    tokens = meta.shape[1]
    hit = meta[:top_k] == lax.axis_index("exp").astype(BF16)
    named = jnp.any(hit, axis=0, keepdims=True)
    gate = jnp.sum(jnp.where(hit, meta[top_k:], 0).astype(F32), axis=0, keepdims=True)
    upto = (jnp.arange(tokens)[:, None] <= jnp.arange(tokens)[None, :]).astype(BF16)
    rank = dot_plain(named.astype(BF16), upto) - 1.0
    chosen = named & (rank == jnp.arange(capacity, dtype=F32)[:, None])
    return hit, chosen, jnp.sum(jnp.where(chosen, gate, 0.0), axis=1, keepdims=True)


def to_replica(value, bit_of_core):
    experts = lax.axis_size("exp")
    pairs = [
        (r * experts + e, (r ^ bit_of_core[e % CORES]) * experts + e)
        for r in range(lax.axis_size("rep"))
        for e in range(experts)
    ]
    return lax.ppermute(value, ("rep", "exp"), pairs)


def on_device(features, out_grad, expert_ids, gate_probs, w_gate, w_up, w_down):
    tokens, model_width = features.shape
    top_k = expert_ids.shape[1]
    hidden_units = w_gate.shape[2]
    experts = lax.axis_size("exp")
    replicas = lax.axis_size("rep")
    chips = experts // CORES
    capacity = min(tokens, 2 * tokens * top_k // experts)
    gate_mat, up_mat, down_mat = (w_gate[0], w_up[0], w_down[0])

    meta = jnp.concatenate([expert_ids.T.astype(BF16), gate_probs.T], axis=0)
    meta = jnp.pad(meta, ((0, EXTRA - 2 * top_k), (0, model_width - tokens)))

    bits = [1 << i for i in range(replicas.bit_length() - 1)]
    turns = list(zip(bits, bits[::-1]))
    own, core = lax.axis_index("rep"), lax.axis_index("exp") % CORES
    shard, half = model_width // replicas, hidden_units // 2
    upper = (own & jnp.where(core == 0, *turns[0])) != 0

    def my_half(value):
        return lax.dynamic_slice_in_dim(value, jnp.where(upper, half, 0), half, axis=1)

    def by_shard(rows):
        cut = []
        for i in range(replicas):
            masks = [sum(turn[c] for j, turn in enumerate(turns) if i >> j & 1) for c in range(CORES)]
            at = (own ^ jnp.where(core == 0, *masks)) * shard
            cut.append(lax.dynamic_slice_in_dim(rows, at, shard, axis=1))
        return jnp.concatenate(cut, axis=1)

    def expert_rows(x, dy, rows_g, weights):
        pre_gate = dot_plain(x, weights[0])
        pre_up = dot_plain(x, weights[1])
        gate_sig = jax.nn.sigmoid(pre_gate)
        gate_act = pre_gate * gate_sig
        hidden = (gate_act * pre_up).astype(BF16)
        back_grad = dot_plain(dy, weights[2])
        scaled = (rows_g * dy.astype(F32)).astype(BF16)
        d_hidden = rows_g * back_grad
        d_gate = d_hidden * pre_up * gate_sig * (1.0 + pre_gate * (1.0 - gate_sig))
        d_up = d_hidden * gate_act
        gate_row = jnp.sum(back_grad * hidden.astype(F32), axis=1, keepdims=True).astype(BF16)
        return scaled, hidden, d_gate.astype(BF16), d_up.astype(BF16), gate_row

    routes, dense = {}, {}

    def pick_x(hop, pair):
        rows = []
        for flip in range(CORES):
            named = pair[flip][tokens : tokens + 2 * top_k, :tokens]
            routes[hop, flip] = route(named, top_k, capacity)
            rows.append(dot_plain(routes[hop, flip][1].astype(BF16), pair[flip][:tokens]))
        return jnp.concatenate(rows, axis=0).astype(BF16)

    def pick_dy(hop, pair):
        rows = [dot_plain(routes[hop, flip][1].astype(BF16), pair[flip]) for flip in range(CORES)]
        rows_g = jnp.concatenate([routes[hop, flip][2] for flip in range(CORES)], axis=0)
        dy = jnp.concatenate(rows, axis=0).astype(BF16)
        gates = jnp.pad(rows_g.astype(BF16).T, ((0, EXTRA - 1), (0, model_width - rows_g.shape[0])))
        return dy, rows_g, jnp.concatenate([dy, gates], axis=0)

    def at_home(x, dy, rows_g):
        scaled, hidden, d_gate, d_up, gate_row = expert_rows(x, dy, rows_g, (gate_mat, up_mat, down_mat))
        terms = (scaled, x, my_half(hidden), my_half(d_gate), my_half(d_up))
        return terms, (d_gate, d_up, gate_row)

    def of_partner(x, block):
        rows = x.shape[0]
        rows_g = block[rows : rows + 1, :rows].T.astype(F32)
        scaled, hidden, d_gate, d_up, _ = expert_rows(x, block[:rows], rows_g, half_mats)
        return scaled, x, hidden, d_gate, d_up

    def sent_back(hops, d_gate, d_up, gate_row):
        row_grad = (dot_last(d_gate, gate_mat) + dot_last(d_up, up_mat)).astype(BF16)
        for place, source in enumerate((hop, flip) for hop in hops for flip in range(CORES)):
            hit, chosen, _ = routes[source]
            mine = slice(place * capacity, (place + 1) * capacity)
            rows = dot_rows(chosen.astype(BF16), row_grad[mine]).astype(BF16)
            value = jnp.where(chosen, gate_row[mine].astype(F32), 0.0)
            gates = jnp.where(hit, jnp.sum(value, axis=0, keepdims=True), 0.0).astype(BF16)
            gates = jnp.pad(gates, ((0, EXTRA - top_k), (0, model_width - tokens)))
            dense[source] = jnp.concatenate([rows, gates], axis=0)

    def joined(groups):
        return [jnp.concatenate(a, axis=0) for a in zip(*groups)]

    kept = max(replicas // 2, CORES) * shard

    def products(terms):
        scaled, x, hidden, d_gate, d_up = terms
        scaled, x = by_shard(scaled), by_shard(x)
        pairs = ((scaled, hidden), (x, d_gate), (x, d_up))
        gone = [dot_rows(left[:, kept:], right) for left, right in pairs]
        return gone, [dot_rows(left[:, :kept], right) for left, right in pairs]

    half_mats = [my_half(value) for value in (gate_mat, up_mat, down_mat)]
    block = jnp.concatenate([features, meta, out_grad], axis=0)
    cut = tokens + EXTRA
    home, partner, back = [], [], []
    for hop in range(chips - 1):
        pair = (block, to_chip(block, experts, 0, 1))
        last = hop + 2 == chips
        moved = to_chip(block[:cut] if last else block, experts, 1, 0)
        x = pick_x(hop, [one[:cut] for one in pair])
        dy, rows_g, with_gates = pick_dy(hop, [one[cut:] for one in pair])
        rows = jnp.concatenate([x, with_gates], axis=0)
        terms, grads = at_home(x, dy, rows_g)
        if last:
            moved, rows, last_dy = lax.optimization_barrier((moved, rows, block[cut:]))
            last_dy = to_chip(last_dy, experts, 1, 0)
        else:
            moved, rows, terms, grads = lax.optimization_barrier((moved, rows, terms, grads))
        block = moved
        shared = to_replica(rows, turns[0])
        home.append(terms)
        partner.append((shared[: x.shape[0]], shared[x.shape[0] :]))
        back.append(grads)
    hop = chips - 1
    sent_back(range(hop), *joined(back))
    gone_early, stay_early = products(joined(home + [of_partner(*p) for p in partner[:-1]]))

    pair_x = (block, to_chip(block, experts, 0, 1))
    gone_early, dense, pair_x = lax.optimization_barrier((gone_early, dense, pair_x))
    x = pick_x(hop, pair_x)
    shared_x = to_replica(x, turns[0])
    pair_dy = (last_dy, to_chip(last_dy, experts, 0, 1))
    dy, rows_g, with_gates = pick_dy(hop, pair_dy)
    shared_dy = to_replica(with_gates, turns[0])
    terms, grads = at_home(x, dy, rows_g)
    gone, stay = products(joined([terms, of_partner(*partner[-1]), of_partner(shared_x, shared_dy)]))
    gone = [(before + after).astype(BF16) for before, after in zip(gone_early, gone)]
    stay = [before + after for before, after in zip(stay_early, stay)]
    def plus(a, b):
        return (a.astype(F32) + b.astype(F32)).astype(BF16)

    def other_core(hops):
        swapped = to_chip(jnp.concatenate([dense[hop, 1] for hop in hops], axis=0), experts, 0, 1)
        return [plus(dense[hop, 0], swapped[i * cut : (i + 1) * cut]) for i, hop in enumerate(hops)]

    summed = other_core(range(chips - 1))
    sent_back([chips - 1], *grads)
    summed += other_core([chips - 1])

    steps = list(range(2, chips + 1))
    in_grad = summed[1 % chips]

    def ring(hops):
        held = in_grad
        for hop in hops:
            held = plus(to_chip(held, experts, 1, 0), summed[hop % chips])
        return held

    deltas = []
    for m in range(3):
        total = stay[m]
        for turn in turns[:0:-1]:
            size = total.shape[0]
            if turn is not turns[-1]:
                size = size // 2
                gone[m], total = total[size:].astype(BF16), total[:size]
            came = to_replica(gone[m], turn)
            if turn is turns[-1]:
                in_grad = ring(steps[m:] if m == 2 else steps[m : m + 1])
                if m < 2:
                    in_grad, came = lax.optimization_barrier((in_grad, came))
            total = total + came.astype(F32)
        total = (total / replicas).astype(BF16)
        mine, came = total[:shard], to_replica(total[shard:], turns[0])
        lower_columns = jnp.where(upper, came, mine)
        upper_columns = jnp.where(upper, mine, came)
        deltas.append(jnp.concatenate([lower_columns, upper_columns], axis=1)[None])
    delta_down, delta_gate, delta_up = deltas
    gate_grad = in_grad[tokens : tokens + top_k, :tokens].T
    return (in_grad[:tokens], gate_grad, delta_gate, delta_up, delta_down)


def solution(mesh):
    by_token = P(("rep", "exp"), None)
    by_expert = P("exp", None, None)
    by_shard = P("exp", "rep", None)
    return jax.shard_map(
        on_device,
        mesh=mesh,
        in_specs=(by_token,) * 4 + (by_expert,) * 3,
        out_specs=(by_token,) * 2 + (by_shard,) * 3,
        check_vma=False,
    )
```

```python
import jax
import jax.numpy as jnp
from jax import lax
from jax.sharding import PartitionSpec as P

F32 = jnp.float32
BF16 = jnp.bfloat16
CORES = 2
EXTRA = 8


def dot_rows(matrix_a, matrix_b):
    return lax.dot_general(
        matrix_a, matrix_b, (((0,), (0,)), ((), ())), preferred_element_type=F32
    )


def dot_last(matrix_a, matrix_b):
    return lax.dot_general(
        matrix_a, matrix_b, (((1,), (1,)), ((), ())), preferred_element_type=F32
    )


def dot_plain(matrix_a, matrix_b):
    return jnp.dot(matrix_a, matrix_b, preferred_element_type=F32)


def to_chip(value, experts, hop, flip):
    chips = experts // CORES
    pairs = [
        (chip * CORES + core, (chip + hop) % chips * CORES + (core ^ flip))
        for chip in range(chips)
        for core in range(CORES)
    ]
    return lax.ppermute(value, "exp", pairs)


def route(meta, top_k, capacity):
    tokens = meta.shape[1]
    hit = meta[:top_k] == lax.axis_index("exp").astype(BF16)
    named = jnp.any(hit, axis=0, keepdims=True)
    gate = jnp.sum(jnp.where(hit, meta[top_k:], 0).astype(F32), axis=0, keepdims=True)
    upto = (jnp.arange(tokens)[:, None] <= jnp.arange(tokens)[None, :]).astype(BF16)
    rank = dot_plain(named.astype(BF16), upto) - 1.0
    chosen = named & (rank == jnp.arange(capacity, dtype=F32)[:, None])
    return hit, chosen, jnp.sum(jnp.where(chosen, gate, 0.0), axis=1, keepdims=True)


def to_replica(value, bit_of_core):
    experts = lax.axis_size("exp")
    pairs = [
        (r * experts + e, (r ^ bit_of_core[e % CORES]) * experts + e)
        for r in range(lax.axis_size("rep"))
        for e in range(experts)
    ]
    return lax.ppermute(value, ("rep", "exp"), pairs)


def on_device(features, out_grad, expert_ids, gate_probs, w_gate, w_up, w_down):
    tokens, model_width = features.shape
    top_k = expert_ids.shape[1]
    hidden_units = w_gate.shape[2]
    experts = lax.axis_size("exp")
    replicas = lax.axis_size("rep")
    chips = experts // CORES
    capacity = min(tokens, 2 * tokens * top_k // experts)
    gate_mat, up_mat, down_mat = (w_gate[0], w_up[0], w_down[0])

    meta = jnp.concatenate([expert_ids.T.astype(BF16), gate_probs.T], axis=0)
    meta = jnp.pad(meta, ((0, EXTRA - 2 * top_k), (0, model_width - tokens)))

    bits = [1 << i for i in range(replicas.bit_length() - 1)]
    turns = list(zip(bits, bits[::-1]))
    own, core = lax.axis_index("rep"), lax.axis_index("exp") % CORES
    shard, half = model_width // replicas, hidden_units // 2
    upper = (own & jnp.where(core == 0, *turns[0])) != 0

    def my_half(value):
        return lax.dynamic_slice_in_dim(value, jnp.where(upper, half, 0), half, axis=1)

    def by_shard(rows):
        cut = []
        for i in range(replicas):
            masks = [sum(turn[c] for j, turn in enumerate(turns) if i >> j & 1) for c in range(CORES)]
            at = (own ^ jnp.where(core == 0, *masks)) * shard
            cut.append(lax.dynamic_slice_in_dim(rows, at, shard, axis=1))
        return jnp.concatenate(cut, axis=1)

    def expert_rows(x, dy, rows_g, weights):
        pre_gate = dot_plain(x, weights[0])
        pre_up = dot_plain(x, weights[1])
        gate_sig = jax.nn.sigmoid(pre_gate)
        gate_act = pre_gate * gate_sig
        hidden = (gate_act * pre_up).astype(BF16)
        back_grad = dot_plain(dy, weights[2])
        scaled = (rows_g * dy.astype(F32)).astype(BF16)
        d_hidden = rows_g * back_grad
        d_gate = d_hidden * pre_up * gate_sig * (1.0 + pre_gate * (1.0 - gate_sig))
        d_up = d_hidden * gate_act
        gate_row = jnp.sum(back_grad * hidden.astype(F32), axis=1, keepdims=True).astype(BF16)
        return scaled, hidden, d_gate.astype(BF16), d_up.astype(BF16), gate_row

    routes, dense = {}, {}

    def pick_x(hop, pair):
        rows = []
        for flip in range(CORES):
            named = pair[flip][tokens : tokens + 2 * top_k, :tokens]
            routes[hop, flip] = route(named, top_k, capacity)
            rows.append(dot_plain(routes[hop, flip][1].astype(BF16), pair[flip][:tokens]))
        return jnp.concatenate(rows, axis=0).astype(BF16)

    def pick_dy(hop, pair):
        rows = [dot_plain(routes[hop, flip][1].astype(BF16), pair[flip]) for flip in range(CORES)]
        rows_g = jnp.concatenate([routes[hop, flip][2] for flip in range(CORES)], axis=0)
        dy = jnp.concatenate(rows, axis=0).astype(BF16)
        gates = jnp.pad(rows_g.astype(BF16).T, ((0, EXTRA - 1), (0, model_width - rows_g.shape[0])))
        return dy, rows_g, jnp.concatenate([dy, gates], axis=0)

    def at_home(x, dy, rows_g):
        scaled, hidden, d_gate, d_up, gate_row = expert_rows(x, dy, rows_g, (gate_mat, up_mat, down_mat))
        terms = (scaled, x, my_half(hidden), my_half(d_gate), my_half(d_up))
        return terms, (d_gate, d_up, gate_row)

    def of_partner(x, block):
        rows = x.shape[0]
        rows_g = block[rows : rows + 1, :rows].T.astype(F32)
        scaled, hidden, d_gate, d_up, _ = expert_rows(x, block[:rows], rows_g, half_mats)
        return scaled, x, hidden, d_gate, d_up

    def sent_back(hops, d_gate, d_up, gate_row):
        row_grad = (dot_last(d_gate, gate_mat) + dot_last(d_up, up_mat)).astype(BF16)
        for place, source in enumerate((hop, flip) for hop in hops for flip in range(CORES)):
            hit, chosen, _ = routes[source]
            mine = slice(place * capacity, (place + 1) * capacity)
            rows = dot_rows(chosen.astype(BF16), row_grad[mine]).astype(BF16)
            value = jnp.where(chosen, gate_row[mine].astype(F32), 0.0)
            gates = jnp.where(hit, jnp.sum(value, axis=0, keepdims=True), 0.0).astype(BF16)
            gates = jnp.pad(gates, ((0, EXTRA - top_k), (0, model_width - tokens)))
            dense[source] = jnp.concatenate([rows, gates], axis=0)

    def joined(groups):
        return [jnp.concatenate(a, axis=0) for a in zip(*groups)]

    kept = max(replicas // 2, CORES) * shard

    def pairs_of(terms):
        scaled, x, hidden, d_gate, d_up = terms
        scaled, x = by_shard(scaled), by_shard(x)
        return [(scaled, hidden), (x, d_gate), (x, d_up)]

    def leaving(pair):
        return dot_rows(pair[0][:, kept:], pair[1])

    def staying(pair):
        return dot_rows(pair[0][:, :kept], pair[1])

    half_mats = [my_half(value) for value in (gate_mat, up_mat, down_mat)]
    block_x, block_dy = jnp.concatenate([features, meta], axis=0), out_grad
    cut = tokens + EXTRA
    home, partner, back = [], [], []
    for hop in range(chips - 1):
        last = hop + 2 == chips
        moved_dy = block_dy if last else to_chip(block_dy, experts, 1, 0)
        moved_x = to_chip(block_x, experts, 1, 0)
        x = pick_x(hop, (block_x, to_chip(block_x, experts, 0, 1)))
        dy, rows_g, with_gates = pick_dy(hop, (block_dy, to_chip(block_dy, experts, 0, 1)))
        rows = jnp.concatenate([x, with_gates], axis=0)
        terms, grads = at_home(x, dy, rows_g)
        moved_x, moved_dy, rows, terms, grads = lax.optimization_barrier(
            (moved_x, moved_dy, rows, terms, grads)
        )
        block_x, block_dy = moved_x, to_chip(moved_dy, experts, 1, 0) if last else moved_dy
        shared = to_replica(rows, turns[0])
        home.append(terms)
        partner.append((shared[: x.shape[0]], shared[x.shape[0] :]))
        back.append(grads)
    hop = chips - 1
    x = pick_x(hop, (block_x, to_chip(block_x, experts, 0, 1)))
    shared_x = to_replica(x, turns[0])
    x, home, back = lax.optimization_barrier((x, home, back))
    sent_back(range(hop), *joined(back))
    pairs = pairs_of(joined(home + [of_partner(*p) for p in partner[:-1]]))
    gone_early, stay_early = [leaving(pair) for pair in pairs], [staying(pair) for pair in pairs]
    gone_early, dense, block_dy, shared_x = lax.optimization_barrier(
        (gone_early, dense, block_dy, shared_x)
    )

    def plus(a, b):
        return (a.astype(F32) + b.astype(F32)).astype(BF16)

    def other_core(hops):
        swapped = to_chip(jnp.concatenate([dense[hop, 1] for hop in hops], axis=0), experts, 0, 1)
        return [plus(dense[hop, 0], swapped[i * cut : (i + 1) * cut]) for i, hop in enumerate(hops)]

    dy, rows_g, with_gates = pick_dy(hop, (block_dy, to_chip(block_dy, experts, 0, 1)))
    shared_dy = to_replica(with_gates, turns[0])
    summed = other_core(range(chips - 1))
    terms, grads = at_home(x, dy, rows_g)
    shared_dy, summed[1 % chips] = lax.optimization_barrier((shared_dy, summed[1 % chips]))
    in_grad = summed[1 % chips]
    steps = list(range(2, chips + 1))

    def ring(held, hops):
        for hop in hops:
            held = plus(to_chip(held, experts, 1, 0), summed[hop % chips])
        return held

    in_grad = ring(in_grad, steps[:1])
    pairs = pairs_of(joined([terms, of_partner(*partner[-1]), of_partner(shared_x, shared_dy)]))
    gone = [(gone_early[m] + leaving(pairs[m])).astype(BF16) for m in range(2)]
    gone, pairs, grads = lax.optimization_barrier((gone, pairs, grads))
    gone.append((gone_early[2] + leaving(pairs[2])).astype(BF16))
    in_grad, gone[2] = lax.optimization_barrier((in_grad, gone[2]))
    stay = [before + staying(pair) for before, pair in zip(stay_early, pairs)]
    sent_back([chips - 1], *grads)
    summed += other_core([chips - 1])

    deltas = []
    for m in range(3):
        total = stay[m]
        for turn in turns[:0:-1]:
            size = total.shape[0]
            if turn is not turns[-1]:
                size = size // 2
                gone[m], total = total[size:].astype(BF16), total[:size]
            came = to_replica(gone[m], turn)
            if turn is turns[-1] and m > 0:
                in_grad = ring(in_grad, steps[1:-1] if m == 1 else steps[1:][-1:])
                in_grad, came = lax.optimization_barrier((in_grad, came))
            total = total + came.astype(F32)
        total = (total / replicas).astype(BF16)
        mine, came = total[:shard], to_replica(total[shard:], turns[0])
        lower_columns = jnp.where(upper, came, mine)
        upper_columns = jnp.where(upper, mine, came)
        deltas.append(jnp.concatenate([lower_columns, upper_columns], axis=1)[None])
    delta_down, delta_gate, delta_up = deltas
    gate_grad = in_grad[tokens : tokens + top_k, :tokens].T
    return (in_grad[:tokens], gate_grad, delta_gate, delta_up, delta_down)


def solution(mesh):
    by_token = P(("rep", "exp"), None)
    by_expert = P("exp", None, None)
    by_shard = P("exp", "rep", None)
    return jax.shard_map(
        on_device,
        mesh=mesh,
        in_specs=(by_token,) * 4 + (by_expert,) * 3,
        out_specs=(by_token,) * 2 + (by_shard,) * 3,
        check_vma=False,
    )
```

```python
import jax
import jax.numpy as jnp
from jax import lax
from jax.sharding import PartitionSpec as P

F32 = jnp.float32
BF16 = jnp.bfloat16
CORES = 2
EXTRA = 8


def dot_rows(matrix_a, matrix_b):
    return lax.dot_general(
        matrix_a, matrix_b, (((0,), (0,)), ((), ())), preferred_element_type=F32
    )


def dot_last(matrix_a, matrix_b):
    return lax.dot_general(
        matrix_a, matrix_b, (((1,), (1,)), ((), ())), preferred_element_type=F32
    )


def dot_plain(matrix_a, matrix_b):
    return jnp.dot(matrix_a, matrix_b, preferred_element_type=F32)


def to_chip(value, experts, hop, flip):
    chips = experts // CORES
    pairs = [
        (chip * CORES + core, (chip + hop) % chips * CORES + (core ^ flip))
        for chip in range(chips)
        for core in range(CORES)
    ]
    return lax.ppermute(value, "exp", pairs)


def route(meta, top_k, capacity):
    tokens = meta.shape[1]
    hit = meta[:top_k] == lax.axis_index("exp").astype(BF16)
    named = jnp.any(hit, axis=0, keepdims=True)
    gate = jnp.sum(jnp.where(hit, meta[top_k:], 0).astype(F32), axis=0, keepdims=True)
    upto = (jnp.arange(tokens)[:, None] <= jnp.arange(tokens)[None, :]).astype(BF16)
    rank = dot_plain(named.astype(BF16), upto) - 1.0
    chosen = named & (rank == jnp.arange(capacity, dtype=F32)[:, None])
    return hit, chosen, jnp.sum(jnp.where(chosen, gate, 0.0), axis=1, keepdims=True)


def to_replica(value, bit_of_core):
    experts = lax.axis_size("exp")
    pairs = [
        (r * experts + e, (r ^ bit_of_core[e % CORES]) * experts + e)
        for r in range(lax.axis_size("rep"))
        for e in range(experts)
    ]
    return lax.ppermute(value, ("rep", "exp"), pairs)


def on_device(features, out_grad, expert_ids, gate_probs, w_gate, w_up, w_down):
    tokens, model_width = features.shape
    top_k = expert_ids.shape[1]
    hidden_units = w_gate.shape[2]
    experts = lax.axis_size("exp")
    replicas = lax.axis_size("rep")
    chips = experts // CORES
    capacity = min(tokens, 2 * tokens * top_k // experts)
    gate_mat, up_mat, down_mat = (w_gate[0], w_up[0], w_down[0])

    meta = jnp.concatenate([expert_ids.T.astype(BF16), gate_probs.T], axis=0)
    meta = jnp.pad(meta, ((0, EXTRA - 2 * top_k), (0, model_width - tokens)))

    bits = [1 << i for i in range(replicas.bit_length() - 1)]
    turns = list(zip(bits, bits[::-1]))
    own, core = lax.axis_index("rep"), lax.axis_index("exp") % CORES
    shard, half = model_width // replicas, hidden_units // 2
    upper = (own & jnp.where(core == 0, *turns[0])) != 0

    def my_half(value):
        return lax.dynamic_slice_in_dim(value, jnp.where(upper, half, 0), half, axis=1)

    def by_shard(rows):
        cut = []
        for i in range(replicas):
            masks = [sum(turn[c] for j, turn in enumerate(turns) if i >> j & 1) for c in range(CORES)]
            at = (own ^ jnp.where(core == 0, *masks)) * shard
            cut.append(lax.dynamic_slice_in_dim(rows, at, shard, axis=1))
        return jnp.concatenate(cut, axis=1)

    def expert_rows(x, dy, rows_g, weights):
        pre_gate = dot_plain(x, weights[0])
        pre_up = dot_plain(x, weights[1])
        gate_sig = jax.nn.sigmoid(pre_gate)
        gate_act = pre_gate * gate_sig
        hidden = (gate_act * pre_up).astype(BF16)
        back_grad = dot_plain(dy, weights[2])
        scaled = (rows_g * dy.astype(F32)).astype(BF16)
        d_hidden = rows_g * back_grad
        d_gate = d_hidden * pre_up * gate_sig * (1.0 + pre_gate * (1.0 - gate_sig))
        d_up = d_hidden * gate_act
        gate_row = jnp.sum(back_grad * hidden.astype(F32), axis=1, keepdims=True).astype(BF16)
        return scaled, hidden, d_gate.astype(BF16), d_up.astype(BF16), gate_row

    routes, dense = {}, {}

    def pick_x(hop, pair):
        rows = []
        for flip in range(CORES):
            named = pair[flip][tokens : tokens + 2 * top_k, :tokens]
            routes[hop, flip] = route(named, top_k, capacity)
            rows.append(dot_plain(routes[hop, flip][1].astype(BF16), pair[flip][:tokens]))
        return jnp.concatenate(rows, axis=0).astype(BF16)

    def pick_dy(hop, pair):
        rows = [dot_plain(routes[hop, flip][1].astype(BF16), pair[flip]) for flip in range(CORES)]
        rows_g = jnp.concatenate([routes[hop, flip][2] for flip in range(CORES)], axis=0)
        dy = jnp.concatenate(rows, axis=0).astype(BF16)
        gates = jnp.pad(rows_g.astype(BF16).T, ((0, EXTRA - 1), (0, model_width - rows_g.shape[0])))
        return dy, rows_g, jnp.concatenate([dy, gates], axis=0)

    def at_home(x, dy, rows_g):
        scaled, hidden, d_gate, d_up, gate_row = expert_rows(x, dy, rows_g, (gate_mat, up_mat, down_mat))
        terms = (scaled, x, my_half(hidden), my_half(d_gate), my_half(d_up))
        return terms, (d_gate, d_up, gate_row)

    def of_partner(x, block):
        rows = x.shape[0]
        rows_g = block[rows : rows + 1, :rows].T.astype(F32)
        scaled, hidden, d_gate, d_up, _ = expert_rows(x, block[:rows], rows_g, half_mats)
        return scaled, x, hidden, d_gate, d_up

    def sent_back(hops, d_gate, d_up, gate_row):
        row_grad = (dot_last(d_gate, gate_mat) + dot_last(d_up, up_mat)).astype(BF16)
        for place, source in enumerate((hop, flip) for hop in hops for flip in range(CORES)):
            hit, chosen, _ = routes[source]
            mine = slice(place * capacity, (place + 1) * capacity)
            rows = dot_rows(chosen.astype(BF16), row_grad[mine]).astype(BF16)
            value = jnp.where(chosen, gate_row[mine].astype(F32), 0.0)
            gates = jnp.where(hit, jnp.sum(value, axis=0, keepdims=True), 0.0).astype(BF16)
            gates = jnp.pad(gates, ((0, EXTRA - top_k), (0, model_width - tokens)))
            dense[source] = jnp.concatenate([rows, gates], axis=0)

    def joined(groups):
        return [jnp.concatenate(a, axis=0) for a in zip(*groups)]

    kept = max(replicas // 2, CORES) * shard

    def pairs_of(terms):
        scaled, x, hidden, d_gate, d_up = terms
        scaled, x = by_shard(scaled), by_shard(x)
        return [(scaled, hidden), (x, d_gate), (x, d_up)]

    def leaving(pair):
        return dot_rows(pair[0][:, kept:], pair[1])

    def staying(pair):
        return dot_rows(pair[0][:, :kept], pair[1])

    def grown(sums, groups):
        pairs = pairs_of(joined(groups))
        gone, stay = [leaving(pair) for pair in pairs], [staying(pair) for pair in pairs]
        if sums:
            gone = [before + after for before, after in zip(sums[0], gone)]
            stay = [before + after for before, after in zip(sums[1], stay)]
        return gone, stay

    def plus(a, b):
        return (a.astype(F32) + b.astype(F32)).astype(BF16)

    def other_core(hops):
        swapped = to_chip(jnp.concatenate([dense[hop, 1] for hop in hops], axis=0), experts, 0, 1)
        return {
            hop: plus(dense[hop, 0], swapped[i * cut : (i + 1) * cut]) for i, hop in enumerate(hops)
        }

    half_mats = [my_half(value) for value in (gate_mat, up_mat, down_mat)]
    block_x, block_dy = jnp.concatenate([features, meta], axis=0), out_grad
    cut = tokens + EXTRA
    home, partner, sums = [], [], ()
    for hop in range(chips - 1):
        last = hop + 2 == chips
        moved_dy = block_dy if last else to_chip(block_dy, experts, 1, 0)
        moved_x = to_chip(block_x, experts, 1, 0)
        x = pick_x(hop, (block_x, to_chip(block_x, experts, 0, 1)))
        dy, rows_g, with_gates = pick_dy(hop, (block_dy, to_chip(block_dy, experts, 0, 1)))
        rows = jnp.concatenate([x, with_gates], axis=0)
        terms, grads = at_home(x, dy, rows_g)
        if last:
            sums = grown(sums, home + [of_partner(*p) for p in partner[:-1]])
        else:
            sent_back([hop], *grads)
        moved_x, moved_dy, rows, terms, grads, dense, sums = lax.optimization_barrier(
            (moved_x, moved_dy, rows, terms, grads, dense, sums)
        )
        block_x, block_dy = moved_x, to_chip(moved_dy, experts, 1, 0) if last else moved_dy
        shared = to_replica(rows, turns[0])
        home.append(terms)
        partner.append((shared[: x.shape[0]], shared[x.shape[0] :]))
    hop = chips - 1
    summed = other_core(range(hop - 1))
    x = pick_x(hop, (block_x, to_chip(block_x, experts, 0, 1)))
    shared_x = to_replica(x, turns[0])
    x, terms, grads = lax.optimization_barrier((x, terms, grads))
    sent_back([hop - 1], *grads)
    sums = grown(sums, [terms, of_partner(*partner[-2])])
    in_grad = summed[1 % chips]
    sums, dense, block_dy, in_grad = lax.optimization_barrier((sums, dense, block_dy, in_grad))

    ring = to_chip(in_grad, experts, 1, 0)
    dy, rows_g, with_gates = pick_dy(hop, (block_dy, to_chip(block_dy, experts, 0, 1)))
    shared_dy = to_replica(with_gates, turns[0])
    summed.update(other_core([hop - 1]))
    terms, grads = at_home(x, dy, rows_g)
    sums = grown(sums, [terms, of_partner(*partner[-1])])
    shared_dy, ring, sums = lax.optimization_barrier((shared_dy, ring, sums))
    in_grad = plus(ring, summed[2 % chips])

    pairs = pairs_of(of_partner(shared_x, shared_dy))
    came = [
        to_replica((before + leaving(pair)).astype(BF16), turns[-1])
        for before, pair in zip(sums[0], pairs)
    ]
    came[0], pairs, grads = lax.optimization_barrier((came[0], pairs, grads))
    sent_back([hop], *grads)
    summed.update(other_core([hop]))
    deltas = []
    for m in range(3):
        if m == 1:
            summed[hop], came[1] = lax.optimization_barrier((summed[hop], came[1]))
            for step in range(3, chips):
                in_grad = plus(to_chip(in_grad, experts, 1, 0), summed[step])
        if m == 2:
            ring, came[2] = lax.optimization_barrier((to_chip(in_grad, experts, 1, 0), came[2]))
            in_grad = plus(ring, summed[0])
        total = sums[1][m] + staying(pairs[m]) + came[m].astype(F32)
        for turn in turns[-2:0:-1]:
            size = total.shape[0] // 2
            total = total[:size] + to_replica(total[size:].astype(BF16), turn).astype(F32)
        total = (total / replicas).astype(BF16)
        mine, other = total[:shard], to_replica(total[shard:], turns[0])
        lower_columns = jnp.where(upper, other, mine)
        upper_columns = jnp.where(upper, mine, other)
        deltas.append(jnp.concatenate([lower_columns, upper_columns], axis=1)[None])
    delta_down, delta_gate, delta_up = deltas
    gate_grad = in_grad[tokens : tokens + top_k, :tokens].T
    return (in_grad[:tokens], gate_grad, delta_gate, delta_up, delta_down)


def solution(mesh):
    by_token = P(("rep", "exp"), None)
    by_expert = P("exp", None, None)
    by_shard = P("exp", "rep", None)
    return jax.shard_map(
        on_device,
        mesh=mesh,
        in_specs=(by_token,) * 4 + (by_expert,) * 3,
        out_specs=(by_token,) * 2 + (by_shard,) * 3,
        check_vma=False,
    )
```

```python
import jax
import jax.numpy as jnp
from jax import lax
from jax.sharding import PartitionSpec as P

F32 = jnp.float32
BF16 = jnp.bfloat16
CORES = 2
EXTRA = 8


def dot_rows(matrix_a, matrix_b):
    return lax.dot_general(
        matrix_a, matrix_b, (((0,), (0,)), ((), ())), preferred_element_type=F32
    )


def dot_last(matrix_a, matrix_b):
    return lax.dot_general(
        matrix_a, matrix_b, (((1,), (1,)), ((), ())), preferred_element_type=F32
    )


def dot_plain(matrix_a, matrix_b):
    return jnp.dot(matrix_a, matrix_b, preferred_element_type=F32)


def to_chip(value, experts, hop, flip):
    chips = experts // CORES
    pairs = [
        (chip * CORES + core, (chip + hop) % chips * CORES + (core ^ flip))
        for chip in range(chips)
        for core in range(CORES)
    ]
    return lax.ppermute(value, "exp", pairs)


def route(meta, top_k, capacity):
    tokens = meta.shape[1]
    hit = meta[:top_k] == lax.axis_index("exp").astype(BF16)
    named = jnp.any(hit, axis=0, keepdims=True)
    gate = jnp.sum(jnp.where(hit, meta[top_k:], 0).astype(F32), axis=0, keepdims=True)
    upto = (jnp.arange(tokens)[:, None] <= jnp.arange(tokens)[None, :]).astype(BF16)
    rank = dot_plain(named.astype(BF16), upto) - 1.0
    chosen = named & (rank == jnp.arange(capacity, dtype=F32)[:, None])
    return hit, chosen, jnp.sum(jnp.where(chosen, gate, 0.0), axis=1, keepdims=True)


def to_replica(value, bit_of_core):
    experts = lax.axis_size("exp")
    pairs = [
        (r * experts + e, (r ^ bit_of_core[e % CORES]) * experts + e)
        for r in range(lax.axis_size("rep"))
        for e in range(experts)
    ]
    return lax.ppermute(value, ("rep", "exp"), pairs)


def on_device(features, out_grad, expert_ids, gate_probs, w_gate, w_up, w_down):
    tokens, model_width = features.shape
    top_k = expert_ids.shape[1]
    experts = lax.axis_size("exp")
    replicas = lax.axis_size("rep")
    chips = experts // CORES
    capacity = min(tokens, 2 * tokens * top_k // experts)
    gate_mat, up_mat, down_mat = (w_gate[0], w_up[0], w_down[0])

    meta = jnp.concatenate([expert_ids.T.astype(BF16), gate_probs.T], axis=0)
    meta = jnp.pad(meta, ((0, EXTRA - 2 * top_k), (0, model_width - tokens)))

    bits = [1 << i for i in range(replicas.bit_length() - 1)]
    turns = list(zip(bits, bits[::-1]))
    own, core = lax.axis_index("rep"), lax.axis_index("exp") % CORES
    shard = model_width // replicas

    def by_shard(rows):
        cut = []
        for i in range(0, replicas, 2):
            masks = [sum(turn[c] for j, turn in enumerate(turns) if i >> j & 1) for c in range(CORES)]
            at = (own ^ jnp.where(core == 0, *masks)) * shard
            cut.append(lax.dynamic_slice_in_dim(rows, at, shard, axis=1))
        return jnp.concatenate(cut, axis=1)

    def expert_rows(x, dy, rows_g):
        pre_gate = dot_plain(x, gate_mat)
        pre_up = dot_plain(x, up_mat)
        gate_sig = jax.nn.sigmoid(pre_gate)
        gate_act = pre_gate * gate_sig
        hidden = (gate_act * pre_up).astype(BF16)
        back_grad = dot_plain(dy, down_mat)
        scaled = (rows_g * dy.astype(F32)).astype(BF16)
        d_hidden = rows_g * back_grad
        d_gate = d_hidden * pre_up * gate_sig * (1.0 + pre_gate * (1.0 - gate_sig))
        d_up = d_hidden * gate_act
        gate_row = jnp.sum(back_grad * hidden.astype(F32), axis=1, keepdims=True).astype(BF16)
        return scaled, hidden, d_gate.astype(BF16), d_up.astype(BF16), gate_row

    routes, dense = {}, {}

    def pick_x(hop, pair):
        rows = []
        for flip in range(CORES):
            named = pair[flip][tokens : tokens + 2 * top_k, :tokens]
            routes[hop, flip] = route(named, top_k, capacity)
            rows.append(dot_plain(routes[hop, flip][1].astype(BF16), pair[flip][:tokens]))
        return jnp.concatenate(rows, axis=0).astype(BF16)

    def pick_dy(hop, pair):
        rows = [dot_plain(routes[hop, flip][1].astype(BF16), pair[flip]) for flip in range(CORES)]
        rows_g = jnp.concatenate([routes[hop, flip][2] for flip in range(CORES)], axis=0)
        dy = jnp.concatenate(rows, axis=0).astype(BF16)
        gates = jnp.pad(rows_g.astype(BF16).T, ((0, EXTRA - 1), (0, model_width - rows_g.shape[0])))
        return dy, rows_g, jnp.concatenate([dy, gates], axis=0)

    def at_home(x, dy, rows_g):
        scaled, hidden, d_gate, d_up, gate_row = expert_rows(x, dy, rows_g)
        return (scaled, x, hidden, d_gate, d_up), (d_gate, d_up, gate_row)

    def of_partner(x, block):
        rows = x.shape[0]
        rows_g = block[rows : rows + 1, :rows].T.astype(F32)
        scaled, hidden, d_gate, d_up, _ = expert_rows(x, block[:rows], rows_g)
        return scaled, x, hidden, d_gate, d_up

    def sent_back(hops, d_gate, d_up, gate_row):
        row_grad = (dot_last(d_gate, gate_mat) + dot_last(d_up, up_mat)).astype(BF16)
        for place, source in enumerate((hop, flip) for hop in hops for flip in range(CORES)):
            hit, chosen, _ = routes[source]
            mine = slice(place * capacity, (place + 1) * capacity)
            rows = dot_rows(chosen.astype(BF16), row_grad[mine]).astype(BF16)
            value = jnp.where(chosen, gate_row[mine].astype(F32), 0.0)
            gates = jnp.where(hit, jnp.sum(value, axis=0, keepdims=True), 0.0).astype(BF16)
            gates = jnp.pad(gates, ((0, EXTRA - top_k), (0, model_width - tokens)))
            dense[source] = jnp.concatenate([rows, gates], axis=0)

    def joined(groups):
        return [jnp.concatenate(a, axis=0) for a in zip(*groups)]

    kept = max(replicas // 4, 1) * shard

    def pairs_of(terms):
        scaled, x, hidden, d_gate, d_up = terms
        scaled, x = by_shard(scaled), by_shard(x)
        return [(scaled, hidden), (x, d_gate), (x, d_up)]

    def leaving(pair):
        return dot_rows(pair[0][:, kept:], pair[1])

    def staying(pair):
        return dot_rows(pair[0][:, :kept], pair[1])

    def grown(sums, groups):
        pairs = pairs_of(joined(groups))
        gone, stay = [leaving(pair) for pair in pairs], [staying(pair) for pair in pairs]
        if sums:
            gone = [before + after for before, after in zip(sums[0], gone)]
            stay = [before + after for before, after in zip(sums[1], stay)]
        return gone, stay

    def plus(a, b):
        return (a.astype(F32) + b.astype(F32)).astype(BF16)

    def other_core(hops):
        swapped = to_chip(jnp.concatenate([dense[hop, 1] for hop in hops], axis=0), experts, 0, 1)
        return {
            hop: plus(dense[hop, 0], swapped[i * cut : (i + 1) * cut]) for i, hop in enumerate(hops)
        }

    block_x, block_dy = jnp.concatenate([features, meta], axis=0), out_grad
    cut = tokens + EXTRA
    home, partner, sums = [], [], ()
    for hop in range(chips - 1):
        last = hop + 2 == chips
        moved_dy = block_dy if last else to_chip(block_dy, experts, 1, 0)
        moved_x = to_chip(block_x, experts, 1, 0)
        x = pick_x(hop, (block_x, to_chip(block_x, experts, 0, 1)))
        dy, rows_g, with_gates = pick_dy(hop, (block_dy, to_chip(block_dy, experts, 0, 1)))
        rows = jnp.concatenate([x, with_gates], axis=0)
        terms, grads = at_home(x, dy, rows_g)
        if last:
            sums = grown(sums, home + [of_partner(*p) for p in partner[:-1]])
        else:
            sent_back([hop], *grads)
        moved_x, moved_dy, rows, terms, grads, dense, sums = lax.optimization_barrier(
            (moved_x, moved_dy, rows, terms, grads, dense, sums)
        )
        block_x, block_dy = moved_x, to_chip(moved_dy, experts, 1, 0) if last else moved_dy
        shared = to_replica(rows, turns[0])
        home.append(terms)
        partner.append((shared[: x.shape[0]], shared[x.shape[0] :]))
    hop = chips - 1
    summed = other_core(range(hop - 1))
    x = pick_x(hop, (block_x, to_chip(block_x, experts, 0, 1)))
    shared_x = to_replica(x, turns[0])
    x, terms, grads = lax.optimization_barrier((x, terms, grads))
    sent_back([hop - 1], *grads)
    sums = grown(sums, [terms, of_partner(*partner[-2])])
    in_grad = summed[1 % chips]
    sums, dense, block_dy, in_grad = lax.optimization_barrier((sums, dense, block_dy, in_grad))

    ring = to_chip(in_grad, experts, 1, 0)
    dy, rows_g, with_gates = pick_dy(hop, (block_dy, to_chip(block_dy, experts, 0, 1)))
    shared_dy = to_replica(with_gates, turns[0])
    summed.update(other_core([hop - 1]))
    shared_x, dy = lax.optimization_barrier((shared_x, dy))
    terms, grads = at_home(x, dy, rows_g)
    sums = grown(sums, [terms, of_partner(*partner[-1])])
    shared_dy, ring, sums = lax.optimization_barrier((shared_dy, ring, sums))

    pairs = pairs_of(of_partner(shared_x, shared_dy))

    def exchanged(m):
        return to_replica((sums[0][m] + leaving(pairs[m])).astype(BF16), turns[-1])

    came = [exchanged(m) for m in range(3)]
    in_grad = plus(ring, summed[2 % chips])
    came[0], pairs, grads = lax.optimization_barrier((came[0], pairs, grads))
    sent_back([hop], *grads)
    summed.update(other_core([hop]))
    deltas = []
    for m in range(3):
        if m == 1:
            summed[hop], came[1] = lax.optimization_barrier((summed[hop], came[1]))
            for step in range(3, chips):
                in_grad = plus(to_chip(in_grad, experts, 1, 0), summed[step])
        total = sums[1][m] + staying(pairs[m]) + came[m].astype(F32)
        for turn in turns[-2:0:-1]:
            size = total.shape[0] // 2
            total = total[:size] + to_replica(total[size:].astype(BF16), turn).astype(F32)
        deltas.append((total / replicas).astype(BF16)[None])
    in_grad = plus(to_chip(in_grad, experts, 1, 0), summed[0])
    delta_down, delta_gate, delta_up = deltas
    gate_grad = in_grad[tokens : tokens + top_k, :tokens].T
    return (in_grad[:tokens], gate_grad, delta_gate, delta_up, delta_down)


def solution(mesh):
    by_token = P(("rep", "exp"), None)
    by_expert = P("exp", None, None)
    by_shard = P("exp", "rep", None)
    return jax.shard_map(
        on_device,
        mesh=mesh,
        in_specs=(by_token,) * 4 + (by_expert,) * 3,
        out_specs=(by_token,) * 2 + (by_shard,) * 3,
        check_vma=False,
    )
```

```python
import jax
import jax.numpy as jnp
from jax import lax
from jax.sharding import PartitionSpec as P

F32 = jnp.float32
BF16 = jnp.bfloat16
CORES = 2
EXTRA = 8


def dot_rows(matrix_a, matrix_b):
    return lax.dot_general(
        matrix_a, matrix_b, (((0,), (0,)), ((), ())), preferred_element_type=F32
    )


def dot_last(matrix_a, matrix_b):
    return lax.dot_general(
        matrix_a, matrix_b, (((1,), (1,)), ((), ())), preferred_element_type=F32
    )


def dot_plain(matrix_a, matrix_b):
    return jnp.dot(matrix_a, matrix_b, preferred_element_type=F32)


def to_chip(value, experts, hop, flip):
    chips = experts // CORES
    pairs = [
        (chip * CORES + core, (chip + hop) % chips * CORES + (core ^ flip))
        for chip in range(chips)
        for core in range(CORES)
    ]
    return lax.ppermute(value, "exp", pairs)


def route(meta, top_k, capacity):
    tokens = meta.shape[1]
    hit = meta[:top_k] == lax.axis_index("exp").astype(BF16)
    named = jnp.any(hit, axis=0, keepdims=True)
    gate = jnp.sum(jnp.where(hit, meta[top_k:], 0).astype(F32), axis=0, keepdims=True)
    upto = (jnp.arange(tokens)[:, None] <= jnp.arange(tokens)[None, :]).astype(BF16)
    rank = dot_plain(named.astype(BF16), upto) - 1.0
    chosen = named & (rank == jnp.arange(capacity, dtype=F32)[:, None])
    return hit, chosen, jnp.sum(jnp.where(chosen, gate, 0.0), axis=1, keepdims=True)


def to_replica(value, bit_of_core):
    experts = lax.axis_size("exp")
    pairs = [
        (r * experts + e, (r ^ bit_of_core[e % CORES]) * experts + e)
        for r in range(lax.axis_size("rep"))
        for e in range(experts)
    ]
    return lax.ppermute(value, ("rep", "exp"), pairs)


def on_device(features, out_grad, expert_ids, gate_probs, w_gate, w_up, w_down):
    tokens, model_width = features.shape
    top_k = expert_ids.shape[1]
    experts = lax.axis_size("exp")
    replicas = lax.axis_size("rep")
    chips = experts // CORES
    capacity = min(tokens, 2 * tokens * top_k // experts)
    gate_mat, up_mat, down_mat = (w_gate[0], w_up[0], w_down[0])

    meta = jnp.concatenate([expert_ids.T.astype(BF16), gate_probs.T], axis=0)
    meta = jnp.pad(meta, ((0, EXTRA - 2 * top_k), (0, model_width - tokens)))

    bits = [1 << i for i in range(replicas.bit_length() - 1)]
    turns = list(zip(bits, bits[::-1]))
    own, core = lax.axis_index("rep"), lax.axis_index("exp") % CORES
    shard = model_width // replicas

    def by_shard(rows):
        cut = []
        for i in range(0, replicas, 2):
            masks = [sum(turn[c] for j, turn in enumerate(turns) if i >> j & 1) for c in range(CORES)]
            at = (own ^ jnp.where(core == 0, *masks)) * shard
            cut.append(lax.dynamic_slice_in_dim(rows, at, shard, axis=1))
        return jnp.concatenate(cut, axis=1)

    def expert_rows(x, dy, rows_g):
        pre_gate = dot_plain(x, gate_mat)
        pre_up = dot_plain(x, up_mat)
        gate_sig = jax.nn.sigmoid(pre_gate)
        gate_act = pre_gate * gate_sig
        hidden = (gate_act * pre_up).astype(BF16)
        back_grad = dot_plain(dy, down_mat)
        scaled = (rows_g * dy.astype(F32)).astype(BF16)
        d_hidden = rows_g * back_grad
        d_gate = d_hidden * pre_up * gate_sig * (1.0 + pre_gate * (1.0 - gate_sig))
        d_up = d_hidden * gate_act
        gate_row = jnp.sum(back_grad * hidden.astype(F32), axis=1, keepdims=True).astype(BF16)
        return scaled, hidden, d_gate.astype(BF16), d_up.astype(BF16), gate_row

    routes, dense = {}, {}

    def pick_x(hop, pair):
        rows = []
        for flip in range(CORES):
            named = pair[flip][tokens : tokens + 2 * top_k, :tokens]
            routes[hop, flip] = route(named, top_k, capacity)
            rows.append(dot_plain(routes[hop, flip][1].astype(BF16), pair[flip][:tokens]))
        return jnp.concatenate(rows, axis=0).astype(BF16)

    def pick_dy(hop, flip, block):
        return dot_plain(routes[hop, flip][1].astype(BF16), block).astype(BF16)

    def gates_of(hop):
        rows_g = jnp.concatenate([routes[hop, flip][2] for flip in range(CORES)], axis=0)
        line = rows_g.astype(BF16).T
        return rows_g, jnp.pad(line, ((0, EXTRA - 1), (0, model_width - line.shape[1])))

    def at_home(x, dy, rows_g):
        scaled, hidden, d_gate, d_up, gate_row = expert_rows(x, dy, rows_g)
        return (scaled, x, hidden, d_gate, d_up), (d_gate, d_up, gate_row)

    def of_partner(with_gates, dy):
        rows = dy.shape[0]
        x, rows_g = with_gates[:rows], with_gates[rows : rows + 1, :rows].T.astype(F32)
        scaled, hidden, d_gate, d_up, _ = expert_rows(x, dy, rows_g)
        return scaled, x, hidden, d_gate, d_up

    def sent_back(hops, d_gate, d_up, gate_row):
        row_grad = (dot_last(d_gate, gate_mat) + dot_last(d_up, up_mat)).astype(BF16)
        for place, source in enumerate((hop, flip) for hop in hops for flip in range(CORES)):
            hit, chosen, _ = routes[source]
            mine = slice(place * capacity, (place + 1) * capacity)
            rows = dot_rows(chosen.astype(BF16), row_grad[mine]).astype(BF16)
            value = jnp.where(chosen, gate_row[mine].astype(F32), 0.0)
            gates = jnp.where(hit, jnp.sum(value, axis=0, keepdims=True), 0.0).astype(BF16)
            gates = jnp.pad(gates, ((0, EXTRA - top_k), (0, model_width - tokens)))
            dense[source] = jnp.concatenate([rows, gates], axis=0)

    def joined(groups):
        return [jnp.concatenate(a, axis=0) for a in zip(*groups)]

    kept = max(replicas // 4, 1) * shard

    def pairs_of(terms):
        scaled, x, hidden, d_gate, d_up = terms
        scaled, x = by_shard(scaled), by_shard(x)
        return [(scaled, hidden), (x, d_gate), (x, d_up)]

    def leaving(pair):
        return dot_rows(pair[0][:, kept:], pair[1])

    def staying(pair):
        return dot_rows(pair[0][:, :kept], pair[1])

    def grown(sums, groups):
        pairs = pairs_of(joined(groups))
        gone, stay = [leaving(pair) for pair in pairs], [staying(pair) for pair in pairs]
        if sums:
            gone = [before + after for before, after in zip(sums[0], gone)]
            stay = [before + after for before, after in zip(sums[1], stay)]
        return gone, stay

    def plus(a, b):
        return (a.astype(F32) + b.astype(F32)).astype(BF16)

    def other_core(hops):
        swapped = to_chip(jnp.concatenate([dense[hop, 1] for hop in hops], axis=0), experts, 0, 1)
        return {
            hop: plus(dense[hop, 0], swapped[i * cut : (i + 1) * cut]) for i, hop in enumerate(hops)
        }

    block_x, block_dy = jnp.concatenate([features, meta], axis=0), out_grad
    cut = tokens + EXTRA
    home, partner, sums = [], [], ()
    for hop in range(chips - 1):
        last = hop + 2 == chips
        moved_dy = block_dy if last else to_chip(block_dy, experts, 1, 0)
        moved_x = to_chip(block_x, experts, 1, 0)
        x = pick_x(hop, (block_x, to_chip(block_x, experts, 0, 1)))
        pair_dy = (block_dy, to_chip(block_dy, experts, 0, 1))
        dy = jnp.concatenate([pick_dy(hop, flip, pair_dy[flip]) for flip in range(CORES)], axis=0)
        rows_g, gates = gates_of(hop)
        rows = jnp.concatenate([x, gates, dy], axis=0)
        terms, grads = at_home(x, dy, rows_g)
        if last:
            sums = grown(sums, home + [of_partner(*p) for p in partner[:-1]])
        else:
            sent_back([hop], *grads)
        moved_x, moved_dy, rows, terms, grads, dense, sums = lax.optimization_barrier(
            (moved_x, moved_dy, rows, terms, grads, dense, sums)
        )
        block_x, block_dy = moved_x, to_chip(moved_dy, experts, 1, 0) if last else moved_dy
        shared = to_replica(rows, turns[0])
        home.append(terms)
        partner.append((shared[: -dy.shape[0]], shared[-dy.shape[0] :]))
    hop = chips - 1
    summed = other_core(range(hop - 1))
    x = pick_x(hop, (block_x, to_chip(block_x, experts, 0, 1)))
    rows_g, gates = gates_of(hop)
    shared_x = to_replica(jnp.concatenate([x, gates], axis=0), turns[0])
    x, terms, grads = lax.optimization_barrier((x, terms, grads))
    sent_back([hop - 1], *grads)
    sums = grown(sums, [terms, of_partner(*partner[-2])])
    in_grad = summed[1 % chips]
    sums, dense, block_dy, in_grad = lax.optimization_barrier((sums, dense, block_dy, in_grad))

    ring = to_chip(in_grad, experts, 1, 0)
    halves = [pick_dy(hop, 0, block_dy)]
    halves.append(pick_dy(hop, 1, to_chip(block_dy, experts, 0, 1)))
    shared_dy = [to_replica(rows, turns[0]) for rows in halves]
    summed.update(other_core([hop - 1]))
    shared_x, halves, partner[-1], shared_dy[0] = lax.optimization_barrier(
        (shared_x, halves, partner[-1], shared_dy[0])
    )
    terms, grads = at_home(x, jnp.concatenate(halves, axis=0), rows_g)
    sums = grown(sums, [terms, of_partner(*partner[-1])])
    shared_dy, sums = lax.optimization_barrier((shared_dy, sums))

    pairs = pairs_of(of_partner(shared_x, jnp.concatenate(shared_dy, axis=0)))

    def exchanged(m):
        return to_replica((sums[0][m] + leaving(pairs[m])).astype(BF16), turns[-1])

    came = [exchanged(0)]
    ring, pairs[1:] = lax.optimization_barrier((ring, pairs[1:]))
    came += [exchanged(1), exchanged(2)]
    in_grad = plus(ring, summed[2 % chips])
    came[0], pairs, grads = lax.optimization_barrier((came[0], pairs, grads))
    sent_back([hop], *grads)
    summed.update(other_core([hop]))
    deltas = []
    for m in range(3):
        if m == 1:
            summed[hop], came[1] = lax.optimization_barrier((summed[hop], came[1]))
            for step in range(3, chips):
                in_grad = plus(to_chip(in_grad, experts, 1, 0), summed[step])
        if m == 2:
            ring, came[2] = lax.optimization_barrier((to_chip(in_grad, experts, 1, 0), came[2]))
        total = sums[1][m] + staying(pairs[m]) + came[m].astype(F32)
        for turn in turns[-2:0:-1]:
            size = total.shape[0] // 2
            total = total[:size] + to_replica(total[size:].astype(BF16), turn).astype(F32)
        deltas.append((total / replicas).astype(BF16)[None])
    in_grad = plus(ring, summed[0])
    delta_down, delta_gate, delta_up = deltas
    gate_grad = in_grad[tokens : tokens + top_k, :tokens].T
    return (in_grad[:tokens], gate_grad, delta_gate, delta_up, delta_down)


def solution(mesh):
    by_token = P(("rep", "exp"), None)
    by_expert = P("exp", None, None)
    by_shard = P("exp", "rep", None)
    return jax.shard_map(
        on_device,
        mesh=mesh,
        in_specs=(by_token,) * 4 + (by_expert,) * 3,
        out_specs=(by_token,) * 2 + (by_shard,) * 3,
        check_vma=False,
    )
```

```python
import jax
import jax.numpy as jnp
from jax import lax
from jax.sharding import PartitionSpec as P

F32 = jnp.float32
BF16 = jnp.bfloat16
CORES = 2
EXTRA = 8


def dot_rows(matrix_a, matrix_b):
    return lax.dot_general(
        matrix_a, matrix_b, (((0,), (0,)), ((), ())), preferred_element_type=F32
    )


def dot_last(matrix_a, matrix_b):
    return lax.dot_general(
        matrix_a, matrix_b, (((1,), (1,)), ((), ())), preferred_element_type=F32
    )


def dot_plain(matrix_a, matrix_b):
    return jnp.dot(matrix_a, matrix_b, preferred_element_type=F32)


def to_chip(value, experts, hop, flip):
    chips = experts // CORES
    pairs = [
        (chip * CORES + core, (chip + hop) % chips * CORES + (core ^ flip))
        for chip in range(chips)
        for core in range(CORES)
    ]
    return lax.ppermute(value, "exp", pairs)


def route(meta, top_k, capacity):
    tokens = meta.shape[1]
    hit = meta[:top_k] == lax.axis_index("exp").astype(BF16)
    named = jnp.any(hit, axis=0, keepdims=True)
    gate = jnp.sum(jnp.where(hit, meta[top_k:], 0).astype(F32), axis=0, keepdims=True)
    upto = (jnp.arange(tokens)[:, None] <= jnp.arange(tokens)[None, :]).astype(BF16)
    rank = dot_plain(named.astype(BF16), upto) - 1.0
    chosen = named & (rank == jnp.arange(capacity, dtype=F32)[:, None])
    return hit, chosen, jnp.sum(jnp.where(chosen, gate, 0.0), axis=1, keepdims=True)


def to_replica(value, bit_of_core):
    experts = lax.axis_size("exp")
    pairs = [
        (r * experts + e, (r ^ bit_of_core[e % CORES]) * experts + e)
        for r in range(lax.axis_size("rep"))
        for e in range(experts)
    ]
    return lax.ppermute(value, ("rep", "exp"), pairs)


def on_device(features, out_grad, expert_ids, gate_probs, w_gate, w_up, w_down):
    tokens, model_width = features.shape
    top_k = expert_ids.shape[1]
    experts = lax.axis_size("exp")
    replicas = lax.axis_size("rep")
    chips = experts // CORES
    capacity = min(tokens, 2 * tokens * top_k // experts)
    gate_mat, up_mat, down_mat = (w_gate[0], w_up[0], w_down[0])

    meta = jnp.concatenate([expert_ids.T.astype(BF16), gate_probs.T], axis=0)
    meta = jnp.pad(meta, ((0, EXTRA - 2 * top_k), (0, model_width - tokens)))

    bits = [1 << i for i in range(replicas.bit_length() - 1)]
    turns = list(zip(bits, bits[::-1]))
    own, core = lax.axis_index("rep"), lax.axis_index("exp") % CORES
    shard = model_width // replicas

    def by_shard(rows):
        cut = []
        for i in range(0, replicas, 2):
            masks = [sum(turn[c] for j, turn in enumerate(turns) if i >> j & 1) for c in range(CORES)]
            at = (own ^ jnp.where(core == 0, *masks)) * shard
            cut.append(lax.dynamic_slice_in_dim(rows, at, shard, axis=1))
        return jnp.concatenate(cut, axis=1)

    def expert_rows(x, dy, rows_g):
        pre_gate = dot_plain(x, gate_mat)
        pre_up = dot_plain(x, up_mat)
        gate_sig = jax.nn.sigmoid(pre_gate)
        gate_act = pre_gate * gate_sig
        hidden = (gate_act * pre_up).astype(BF16)
        back_grad = dot_plain(dy, down_mat)
        scaled = (rows_g * dy.astype(F32)).astype(BF16)
        d_hidden = rows_g * back_grad
        d_gate = d_hidden * pre_up * gate_sig * (1.0 + pre_gate * (1.0 - gate_sig))
        d_up = d_hidden * gate_act
        gate_row = jnp.sum(back_grad * hidden.astype(F32), axis=1, keepdims=True).astype(BF16)
        return scaled, hidden, d_gate.astype(BF16), d_up.astype(BF16), gate_row

    routes, dense = {}, {}

    def pick_x(hop, pair):
        rows = []
        for flip in range(CORES):
            named = pair[flip][tokens : tokens + 2 * top_k, :tokens]
            routes[hop, flip] = route(named, top_k, capacity)
            rows.append(dot_plain(routes[hop, flip][1].astype(BF16), pair[flip][:tokens]))
        return jnp.concatenate(rows, axis=0).astype(BF16)

    def pick_dy(hop, flip, block):
        return dot_plain(routes[hop, flip][1].astype(BF16), block).astype(BF16)

    def gates_of(hop):
        rows_g = jnp.concatenate([routes[hop, flip][2] for flip in range(CORES)], axis=0)
        line = rows_g.astype(BF16).T
        return rows_g, jnp.pad(line, ((0, EXTRA - 1), (0, model_width - line.shape[1])))

    def at_home(x, dy, rows_g):
        scaled, hidden, d_gate, d_up, gate_row = expert_rows(x, dy, rows_g)
        return (scaled, x, hidden, d_gate, d_up), (d_gate, d_up, gate_row)

    def of_partner(with_gates, dy):
        rows = dy.shape[0]
        x, rows_g = with_gates[:rows], with_gates[rows : rows + 1, :rows].T.astype(F32)
        scaled, hidden, d_gate, d_up, _ = expert_rows(x, dy, rows_g)
        return scaled, x, hidden, d_gate, d_up

    def sent_back(hops, d_gate, d_up, gate_row):
        row_grad = (dot_last(d_gate, gate_mat) + dot_last(d_up, up_mat)).astype(BF16)
        for place, source in enumerate((hop, flip) for hop in hops for flip in range(CORES)):
            hit, chosen, _ = routes[source]
            mine = slice(place * capacity, (place + 1) * capacity)
            rows = dot_rows(chosen.astype(BF16), row_grad[mine]).astype(BF16)
            value = jnp.where(chosen, gate_row[mine].astype(F32), 0.0)
            gates = jnp.where(hit, jnp.sum(value, axis=0, keepdims=True), 0.0).astype(BF16)
            gates = jnp.pad(gates, ((0, EXTRA - top_k), (0, model_width - tokens)))
            dense[source] = jnp.concatenate([rows, gates], axis=0)

    def joined(groups):
        return [jnp.concatenate(a, axis=0) for a in zip(*groups)]

    kept = max(replicas // 4, 1) * shard

    def pairs_of(terms):
        scaled, x, hidden, d_gate, d_up = terms
        scaled, x = by_shard(scaled), by_shard(x)
        return [(scaled, hidden), (x, d_gate), (x, d_up)]

    def leaving(pair):
        return dot_rows(pair[0][:, kept:], pair[1])

    def staying(pair):
        return dot_rows(pair[0][:, :kept], pair[1])

    def grown(sums, groups):
        pairs = pairs_of(joined(groups))
        gone, stay = [leaving(pair) for pair in pairs], [staying(pair) for pair in pairs]
        if sums:
            gone = [before + after for before, after in zip(sums[0], gone)]
            stay = [before + after for before, after in zip(sums[1], stay)]
        return gone, stay

    def plus(a, b):
        return (a.astype(F32) + b.astype(F32)).astype(BF16)

    def other_core(hops):
        swapped = to_chip(jnp.concatenate([dense[hop, 1] for hop in hops], axis=0), experts, 0, 1)
        return {
            hop: plus(dense[hop, 0], swapped[i * cut : (i + 1) * cut]) for i, hop in enumerate(hops)
        }

    block_x, block_dy = jnp.concatenate([features, meta], axis=0), out_grad
    cut = tokens + EXTRA
    home, partner, sums = [], [], ()
    for hop in range(chips - 1):
        last = hop + 2 == chips
        moved_dy = block_dy if last else to_chip(block_dy, experts, 1, 0)
        moved_x = to_chip(block_x, experts, 1, 0)
        x = pick_x(hop, (block_x, to_chip(block_x, experts, 0, 1)))
        pair_dy = (block_dy, to_chip(block_dy, experts, 0, 1))
        dy = jnp.concatenate([pick_dy(hop, flip, pair_dy[flip]) for flip in range(CORES)], axis=0)
        rows_g, gates = gates_of(hop)
        rows = jnp.concatenate([x, gates, dy], axis=0)
        terms, grads = at_home(x, dy, rows_g)
        if last:
            sums = grown(sums, home + [of_partner(*p) for p in partner[:-1]])
        else:
            sent_back([hop], *grads)
        moved_x, moved_dy, rows, terms, grads, dense, sums = lax.optimization_barrier(
            (moved_x, moved_dy, rows, terms, grads, dense, sums)
        )
        block_x, block_dy = moved_x, to_chip(moved_dy, experts, 1, 0) if last else moved_dy
        shared = to_replica(rows, turns[0])
        home.append(terms)
        partner.append((shared[: -dy.shape[0]], shared[-dy.shape[0] :]))
    hop = chips - 1
    summed = other_core(range(hop - 1))
    x = pick_x(hop, (block_x, to_chip(block_x, experts, 0, 1)))
    rows_g, gates = gates_of(hop)
    shared_x = to_replica(jnp.concatenate([x, gates], axis=0), turns[0])
    x, terms, grads = lax.optimization_barrier((x, terms, grads))
    sent_back([hop - 1], *grads)
    sums = grown(sums, [terms, of_partner(*partner[-2])])
    in_grad = summed[1 % chips]
    sums, dense, block_dy, in_grad = lax.optimization_barrier((sums, dense, block_dy, in_grad))

    ring = to_chip(in_grad, experts, 1, 0)
    halves = [pick_dy(hop, 0, block_dy)]
    halves.append(pick_dy(hop, 1, to_chip(block_dy, experts, 0, 1)))
    shared_dy = [to_replica(rows, turns[0]) for rows in halves]
    summed.update(other_core([hop - 1]))
    shared_x, halves, partner[-1], shared_dy[0] = lax.optimization_barrier(
        (shared_x, halves, partner[-1], shared_dy[0])
    )
    terms, grads = at_home(x, jnp.concatenate(halves, axis=0), rows_g)
    sums = grown(sums, [terms, of_partner(*partner[-1])])
    shared_dy, sums = lax.optimization_barrier((shared_dy, sums))

    pairs = pairs_of(of_partner(shared_x, jnp.concatenate(shared_dy, axis=0)))

    def product(m):
        return (sums[0][m] + leaving(pairs[m])).astype(BF16)

    came = [to_replica(product(0), turns[-1])]
    in_grad = plus(ring, summed[2 % chips])
    in_grad, pairs[1:] = lax.optimization_barrier((in_grad, pairs[1:]))
    came.append(to_replica(product(1), turns[-1]))
    gone, grads = lax.optimization_barrier((product(2), grads))
    came.append(to_replica(gone, turns[-1]))
    sent_back([hop], *grads)
    summed.update(other_core([hop]))
    for step in range(3, chips):
        ring = to_chip(in_grad, experts, 1, 0)
        if step == 3:
            came[0], pairs, ring = lax.optimization_barrier((came[0], pairs, ring))
        in_grad = plus(ring, summed[step])
    ring, came[2] = lax.optimization_barrier((to_chip(in_grad, experts, 1, 0), came[2]))
    in_grad = plus(ring, summed[0])
    deltas = []
    for m in range(3):
        total = sums[1][m] + staying(pairs[m]) + came[m].astype(F32)
        for turn in turns[-2:0:-1]:
            size = total.shape[0] // 2
            total = total[:size] + to_replica(total[size:].astype(BF16), turn).astype(F32)
        deltas.append((total / replicas).astype(BF16)[None])
    delta_down, delta_gate, delta_up = deltas
    gate_grad = in_grad[tokens : tokens + top_k, :tokens].T
    return (in_grad[:tokens], gate_grad, delta_gate, delta_up, delta_down)


def solution(mesh):
    by_token = P(("rep", "exp"), None)
    by_expert = P("exp", None, None)
    by_shard = P("exp", "rep", None)
    return jax.shard_map(
        on_device,
        mesh=mesh,
        in_specs=(by_token,) * 4 + (by_expert,) * 3,
        out_specs=(by_token,) * 2 + (by_shard,) * 3,
        check_vma=False,
    )
```

```python
import jax
import jax.numpy as jnp
from jax import lax
from jax.sharding import PartitionSpec as P

F32 = jnp.float32
BF16 = jnp.bfloat16
CORES = 2
EXTRA = 8


def dot_rows(matrix_a, matrix_b):
    return lax.dot_general(
        matrix_a, matrix_b, (((0,), (0,)), ((), ())), preferred_element_type=F32
    )


def dot_last(matrix_a, matrix_b):
    return lax.dot_general(
        matrix_a, matrix_b, (((1,), (1,)), ((), ())), preferred_element_type=F32
    )


def dot_plain(matrix_a, matrix_b):
    return jnp.dot(matrix_a, matrix_b, preferred_element_type=F32)


def to_chip(value, experts, hop, flip):
    chips = experts // CORES
    pairs = [
        (chip * CORES + core, (chip + hop) % chips * CORES + (core ^ flip))
        for chip in range(chips)
        for core in range(CORES)
    ]
    return lax.ppermute(value, "exp", pairs)


def route(meta, top_k, capacity):
    tokens = meta.shape[1]
    hit = meta[:top_k] == lax.axis_index("exp").astype(BF16)
    named = jnp.any(hit, axis=0, keepdims=True)
    gate = jnp.sum(jnp.where(hit, meta[top_k:], 0).astype(F32), axis=0, keepdims=True)
    upto = (jnp.arange(tokens)[:, None] <= jnp.arange(tokens)[None, :]).astype(BF16)
    rank = dot_plain(named.astype(BF16), upto) - 1.0
    chosen = named & (rank == jnp.arange(capacity, dtype=F32)[:, None])
    return hit, chosen, jnp.sum(jnp.where(chosen, gate, 0.0), axis=1, keepdims=True)


def to_replica(value, bit_of_core):
    experts = lax.axis_size("exp")
    pairs = [
        (r * experts + e, (r ^ bit_of_core[e % CORES]) * experts + e)
        for r in range(lax.axis_size("rep"))
        for e in range(experts)
    ]
    return lax.ppermute(value, ("rep", "exp"), pairs)


def on_device(features, out_grad, expert_ids, gate_probs, w_gate, w_up, w_down):
    tokens, model_width = features.shape
    top_k = expert_ids.shape[1]
    experts = lax.axis_size("exp")
    replicas = lax.axis_size("rep")
    chips = experts // CORES
    capacity = min(tokens, 2 * tokens * top_k // experts)
    gate_mat, up_mat, down_mat = (w_gate[0], w_up[0], w_down[0])

    meta = jnp.concatenate([expert_ids.T.astype(BF16), gate_probs.T], axis=0)
    meta = jnp.pad(meta, ((0, EXTRA - 2 * top_k), (0, model_width - tokens)))

    bits = [1 << i for i in range(replicas.bit_length() - 1)]
    turns = list(zip(bits, bits[::-1]))
    own, core = lax.axis_index("rep"), lax.axis_index("exp") % CORES
    shard = model_width // replicas

    def by_shard(rows):
        cut = []
        for i in range(0, replicas, 2):
            masks = [sum(turn[c] for j, turn in enumerate(turns) if i >> j & 1) for c in range(CORES)]
            at = (own ^ jnp.where(core == 0, *masks)) * shard
            cut.append(lax.dynamic_slice_in_dim(rows, at, shard, axis=1))
        return jnp.concatenate(cut, axis=1)

    def expert_rows(x, dy, rows_g):
        pre_gate = dot_plain(x, gate_mat)
        pre_up = dot_plain(x, up_mat)
        gate_sig = jax.nn.sigmoid(pre_gate)
        gate_act = pre_gate * gate_sig
        hidden = (gate_act * pre_up).astype(BF16)
        back_grad = dot_plain(dy, down_mat)
        scaled = (rows_g * dy.astype(F32)).astype(BF16)
        d_hidden = rows_g * back_grad
        d_gate = d_hidden * pre_up * gate_sig * (1.0 + pre_gate * (1.0 - gate_sig))
        d_up = d_hidden * gate_act
        gate_row = jnp.sum(back_grad * hidden.astype(F32), axis=1, keepdims=True).astype(BF16)
        return scaled, hidden, d_gate.astype(BF16), d_up.astype(BF16), gate_row

    routes, dense = {}, {}

    def pick_x(hop, pair):
        rows = []
        for flip in range(CORES):
            named = pair[flip][tokens : tokens + 2 * top_k, :tokens]
            routes[hop, flip] = route(named, top_k, capacity)
            rows.append(dot_plain(routes[hop, flip][1].astype(BF16), pair[flip][:tokens]))
        return jnp.concatenate(rows, axis=0).astype(BF16)

    def pick_dy(hop, flip, block):
        return dot_plain(routes[hop, flip][1].astype(BF16), block).astype(BF16)

    def gates_of(hop):
        rows_g = jnp.concatenate([routes[hop, flip][2] for flip in range(CORES)], axis=0)
        line = rows_g.astype(BF16).T
        return rows_g, jnp.pad(line, ((0, EXTRA - 1), (0, model_width - line.shape[1])))

    def at_home(x, dy, rows_g):
        scaled, hidden, d_gate, d_up, gate_row = expert_rows(x, dy, rows_g)
        return (scaled, x, hidden, d_gate, d_up), (d_gate, d_up, gate_row)

    def of_partner(with_gates, dy):
        rows = dy.shape[0]
        x, rows_g = with_gates[:rows], with_gates[rows : rows + 1, :rows].T.astype(F32)
        scaled, hidden, d_gate, d_up, _ = expert_rows(x, dy, rows_g)
        return scaled, x, hidden, d_gate, d_up

    def sent_back(hops, d_gate, d_up, gate_row):
        row_grad = (dot_last(d_gate, gate_mat) + dot_last(d_up, up_mat)).astype(BF16)
        for place, source in enumerate((hop, flip) for hop in hops for flip in range(CORES)):
            hit, chosen, _ = routes[source]
            mine = slice(place * capacity, (place + 1) * capacity)
            rows = dot_rows(chosen.astype(BF16), row_grad[mine]).astype(BF16)
            value = jnp.where(chosen, gate_row[mine].astype(F32), 0.0)
            gates = jnp.where(hit, jnp.sum(value, axis=0, keepdims=True), 0.0).astype(BF16)
            gates = jnp.pad(gates, ((0, EXTRA - top_k), (0, model_width - tokens)))
            dense[source] = jnp.concatenate([rows, gates], axis=0)

    def joined(groups):
        return [jnp.concatenate(a, axis=0) for a in zip(*groups)]

    kept = max(replicas // 4, 1) * shard

    def pairs_of(terms):
        scaled, x, hidden, d_gate, d_up = terms
        scaled, x = by_shard(scaled), by_shard(x)
        return [(scaled, hidden), (x, d_gate), (x, d_up)]

    def leaving(pair):
        return dot_rows(pair[0][:, kept:], pair[1])

    def staying(pair):
        return dot_rows(pair[0][:, :kept], pair[1])

    def grown(sums, groups):
        pairs = pairs_of(joined(groups))
        gone, stay = [leaving(pair) for pair in pairs], [staying(pair) for pair in pairs]
        if sums:
            gone = [before + after for before, after in zip(sums[0], gone)]
            stay = [before + after for before, after in zip(sums[1], stay)]
        return gone, stay

    def plus(a, b):
        return (a.astype(F32) + b.astype(F32)).astype(BF16)

    def other_core(hops):
        swapped = to_chip(jnp.concatenate([dense[hop, 1] for hop in hops], axis=0), experts, 0, 1)
        return {
            hop: plus(dense[hop, 0], swapped[i * cut : (i + 1) * cut]) for i, hop in enumerate(hops)
        }

    block_dy = out_grad
    other_dy, meta = lax.optimization_barrier((to_chip(out_grad, experts, 0, 1), meta))
    block_x = jnp.concatenate([features, meta], axis=0)
    cut = tokens + EXTRA
    home, partner, sums = [], [], ()
    for hop in range(chips - 1):
        last = hop + 2 == chips
        moved_x = to_chip(block_x, experts, 1, 0)
        moved_dy = to_chip(block_dy, experts, 1, 0)
        x = pick_x(hop, (block_x, to_chip(block_x, experts, 0, 1)))
        pair_dy = (block_dy, other_dy if hop == 0 else to_chip(block_dy, experts, 0, 1))
        dy = jnp.concatenate([pick_dy(hop, flip, pair_dy[flip]) for flip in range(CORES)], axis=0)
        rows_g, gates = gates_of(hop)
        rows = jnp.concatenate([x, gates, dy], axis=0)
        terms, grads = at_home(x, dy, rows_g)
        if last:
            sums = grown(sums, home + [of_partner(*p) for p in partner[:-1]])
        else:
            sent_back([hop], *grads)
        moved_x, rows, terms, grads, dense, sums = lax.optimization_barrier(
            (moved_x, rows, terms, grads, dense, sums)
        )
        if not last:
            moved_x, moved_dy = lax.optimization_barrier((moved_x, moved_dy))
        block_x, block_dy = moved_x, moved_dy
        shared = to_replica(rows, turns[0])
        home.append(terms)
        partner.append((shared[: -dy.shape[0]], shared[-dy.shape[0] :]))
    hop = chips - 1
    summed = other_core(range(hop - 1))
    x = pick_x(hop, (block_x, to_chip(block_x, experts, 0, 1)))
    rows_g, gates = gates_of(hop)
    shared_x = to_replica(jnp.concatenate([x, gates], axis=0), turns[0])
    x, terms, grads = lax.optimization_barrier((x, terms, grads))
    sent_back([hop - 1], *grads)
    sums = grown(sums, [terms, of_partner(*partner[-2])])
    in_grad = summed[1 % chips]
    sums, dense, block_dy, in_grad = lax.optimization_barrier((sums, dense, block_dy, in_grad))

    ring = to_chip(in_grad, experts, 1, 0)
    halves = [pick_dy(hop, 0, block_dy)]
    halves.append(pick_dy(hop, 1, to_chip(block_dy, experts, 0, 1)))
    shared_dy = [to_replica(rows, turns[0]) for rows in halves]
    summed.update(other_core([hop - 1]))
    shared_x, halves, partner[-1], shared_dy[0] = lax.optimization_barrier(
        (shared_x, halves, partner[-1], shared_dy[0])
    )
    terms, grads = at_home(x, jnp.concatenate(halves, axis=0), rows_g)
    sums = grown(sums, [terms, of_partner(*partner[-1])])
    shared_dy, sums = lax.optimization_barrier((shared_dy, sums))

    pairs = pairs_of(of_partner(shared_x, jnp.concatenate(shared_dy, axis=0)))

    def product(m):
        return (sums[0][m] + leaving(pairs[m])).astype(BF16)

    came = [to_replica(product(0), turns[-1])]
    in_grad = plus(ring, summed[2 % chips])
    in_grad, pairs[1:] = lax.optimization_barrier((in_grad, pairs[1:]))
    came.append(to_replica(product(1), turns[-1]))
    gone, grads = lax.optimization_barrier((product(2), grads))
    came.append(to_replica(gone, turns[-1]))
    sent_back([hop], *grads)
    summed.update(other_core([hop]))
    for step in range(3, chips):
        ring = to_chip(in_grad, experts, 1, 0)
        if step == 3:
            came[0], pairs, ring = lax.optimization_barrier((came[0], pairs, ring))
        in_grad = plus(ring, summed[step])
    ring, came[2] = lax.optimization_barrier((to_chip(in_grad, experts, 1, 0), came[2]))
    in_grad = plus(ring, summed[0])
    deltas = []
    for m in range(3):
        total = sums[1][m] + staying(pairs[m]) + came[m].astype(F32)
        for turn in turns[-2:0:-1]:
            size = total.shape[0] // 2
            total = total[:size] + to_replica(total[size:].astype(BF16), turn).astype(F32)
        deltas.append((total / replicas).astype(BF16)[None])
    delta_down, delta_gate, delta_up = deltas
    gate_grad = in_grad[tokens : tokens + top_k, :tokens].T
    return (in_grad[:tokens], gate_grad, delta_gate, delta_up, delta_down)


def solution(mesh):
    by_token = P(("rep", "exp"), None)
    by_expert = P("exp", None, None)
    by_shard = P("exp", "rep", None)
    return jax.shard_map(
        on_device,
        mesh=mesh,
        in_specs=(by_token,) * 4 + (by_expert,) * 3,
        out_specs=(by_token,) * 2 + (by_shard,) * 3,
        check_vma=False,
    )
```

```python
import jax
import jax.numpy as jnp
from jax import lax
from jax.sharding import PartitionSpec as P

F32 = jnp.float32
BF16 = jnp.bfloat16
CORES = 2
EXTRA = 8


def dot_rows(matrix_a, matrix_b):
    return lax.dot_general(
        matrix_a, matrix_b, (((0,), (0,)), ((), ())), preferred_element_type=F32
    )


def dot_last(matrix_a, matrix_b):
    return lax.dot_general(
        matrix_a, matrix_b, (((1,), (1,)), ((), ())), preferred_element_type=F32
    )


def dot_plain(matrix_a, matrix_b):
    return jnp.dot(matrix_a, matrix_b, preferred_element_type=F32)


def to_chip(value, experts, hop, flip):
    chips = experts // CORES
    pairs = [
        (chip * CORES + core, (chip + hop) % chips * CORES + (core ^ flip))
        for chip in range(chips)
        for core in range(CORES)
    ]
    return lax.ppermute(value, "exp", pairs)


def route(meta, top_k, capacity):
    tokens = meta.shape[1]
    hit = meta[:top_k] == lax.axis_index("exp").astype(BF16)
    named = jnp.any(hit, axis=0, keepdims=True)
    gate = jnp.sum(jnp.where(hit, meta[top_k:], 0).astype(F32), axis=0, keepdims=True)
    upto = (jnp.arange(tokens)[:, None] <= jnp.arange(tokens)[None, :]).astype(BF16)
    rank = dot_plain(named.astype(BF16), upto) - 1.0
    chosen = named & (rank == jnp.arange(capacity, dtype=F32)[:, None])
    return hit, chosen, jnp.sum(jnp.where(chosen, gate, 0.0), axis=1, keepdims=True)


def to_replica(value, bit_of_core):
    experts = lax.axis_size("exp")
    pairs = [
        (r * experts + e, (r ^ bit_of_core[e % CORES]) * experts + e)
        for r in range(lax.axis_size("rep"))
        for e in range(experts)
    ]
    return lax.ppermute(value, ("rep", "exp"), pairs)


def on_device(features, out_grad, expert_ids, gate_probs, w_gate, w_up, w_down):
    tokens, model_width = features.shape
    top_k = expert_ids.shape[1]
    experts = lax.axis_size("exp")
    replicas = lax.axis_size("rep")
    chips = experts // CORES
    capacity = min(tokens, 2 * tokens * top_k // experts)
    gate_mat, up_mat, down_mat = (w_gate[0], w_up[0], w_down[0])

    meta = jnp.concatenate([expert_ids.T.astype(BF16), gate_probs.T], axis=0)
    meta = jnp.pad(meta, ((0, EXTRA - 2 * top_k), (0, model_width - tokens)))

    bits = [1 << i for i in range(replicas.bit_length() - 1)]
    turns = list(zip(bits, bits[::-1]))
    own, core = lax.axis_index("rep"), lax.axis_index("exp") % CORES
    shard = model_width // replicas

    def by_shard(rows):
        cut = []
        for i in range(0, replicas, 2):
            masks = [sum(turn[c] for j, turn in enumerate(turns) if i >> j & 1) for c in range(CORES)]
            at = (own ^ jnp.where(core == 0, *masks)) * shard
            cut.append(lax.dynamic_slice_in_dim(rows, at, shard, axis=1))
        return jnp.concatenate(cut, axis=1)

    def expert_rows(x, dy, rows_g):
        pre_gate = dot_plain(x, gate_mat)
        pre_up = dot_plain(x, up_mat)
        gate_sig = jax.nn.sigmoid(pre_gate)
        gate_act = pre_gate * gate_sig
        hidden = (gate_act * pre_up).astype(BF16)
        back_grad = dot_plain(dy, down_mat)
        scaled = (rows_g * dy.astype(F32)).astype(BF16)
        d_hidden = rows_g * back_grad
        d_gate = d_hidden * pre_up * gate_sig * (1.0 + pre_gate * (1.0 - gate_sig))
        d_up = d_hidden * gate_act
        gate_row = jnp.sum(back_grad * hidden.astype(F32), axis=1, keepdims=True).astype(BF16)
        return scaled, hidden, d_gate.astype(BF16), d_up.astype(BF16), gate_row

    routes, dense = {}, {}

    def pick_x(hop, pair):
        rows = []
        for flip in range(CORES):
            named = pair[flip][tokens : tokens + 2 * top_k, :tokens]
            routes[hop, flip] = route(named, top_k, capacity)
            rows.append(dot_plain(routes[hop, flip][1].astype(BF16), pair[flip][:tokens]))
        return jnp.concatenate(rows, axis=0).astype(BF16)

    def pick_dy(hop, flip, block):
        return dot_plain(routes[hop, flip][1].astype(BF16), block).astype(BF16)

    def gates_of(hop):
        rows_g = jnp.concatenate([routes[hop, flip][2] for flip in range(CORES)], axis=0)
        line = rows_g.astype(BF16).T
        return rows_g, jnp.pad(line, ((0, EXTRA - 1), (0, model_width - line.shape[1])))

    def at_home(x, dy, rows_g):
        scaled, hidden, d_gate, d_up, gate_row = expert_rows(x, dy, rows_g)
        return (scaled, x, hidden, d_gate, d_up), (d_gate, d_up, gate_row)

    def of_partner(with_gates, dy):
        rows = dy.shape[0]
        x, rows_g = with_gates[:rows], with_gates[rows : rows + 1, :rows].T.astype(F32)
        scaled, hidden, d_gate, d_up, _ = expert_rows(x, dy, rows_g)
        return scaled, x, hidden, d_gate, d_up

    def sent_back(hops, d_gate, d_up, gate_row):
        row_grad = (dot_last(d_gate, gate_mat) + dot_last(d_up, up_mat)).astype(BF16)
        for place, source in enumerate((hop, flip) for hop in hops for flip in range(CORES)):
            hit, chosen, _ = routes[source]
            mine = slice(place * capacity, (place + 1) * capacity)
            rows = dot_rows(chosen.astype(BF16), row_grad[mine]).astype(BF16)
            value = jnp.where(chosen, gate_row[mine].astype(F32), 0.0)
            gates = jnp.where(hit, jnp.sum(value, axis=0, keepdims=True), 0.0).astype(BF16)
            gates = jnp.pad(gates, ((0, EXTRA - top_k), (0, model_width - tokens)))
            dense[source] = jnp.concatenate([rows, gates], axis=0)

    def joined(groups):
        return [jnp.concatenate(a, axis=0) for a in zip(*groups)]

    kept = max(replicas // 4, 1) * shard

    def pairs_of(terms):
        scaled, x, hidden, d_gate, d_up = terms
        scaled, x = by_shard(scaled), by_shard(x)
        return [(scaled, hidden), (x, d_gate), (x, d_up)]

    def leaving(pair):
        return dot_rows(pair[0][:, kept:], pair[1])

    def staying(pair):
        return dot_rows(pair[0][:, :kept], pair[1])

    def grown(sums, groups):
        pairs = pairs_of(joined(groups))
        gone, stay = [leaving(pair) for pair in pairs], [staying(pair) for pair in pairs]
        if sums:
            gone = [before + after for before, after in zip(sums[0], gone)]
            stay = [before + after for before, after in zip(sums[1], stay)]
        return gone, stay

    def plus(a, b):
        return (a.astype(F32) + b.astype(F32)).astype(BF16)

    def other_core(hops):
        swapped = to_chip(jnp.concatenate([dense[hop, 1] for hop in hops], axis=0), experts, 0, 1)
        return {
            hop: plus(dense[hop, 0], swapped[i * cut : (i + 1) * cut]) for i, hop in enumerate(hops)
        }

    block_dy = out_grad
    other_dy, meta = lax.optimization_barrier((to_chip(out_grad, experts, 0, 1), meta))
    block_x = jnp.concatenate([features, meta], axis=0)
    cut = tokens + EXTRA
    home, partner, sums = [], [], ()
    for hop in range(chips - 1):
        last = hop + 2 == chips
        moved_x = to_chip(block_x, experts, 1, 0)
        moved_dy = block_dy if last else to_chip(block_dy, experts, 1, 0)
        x = pick_x(hop, (block_x, to_chip(block_x, experts, 0, 1)))
        pair_dy = (block_dy, other_dy if hop == 0 else to_chip(block_dy, experts, 0, 1))
        dy = jnp.concatenate([pick_dy(hop, flip, pair_dy[flip]) for flip in range(CORES)], axis=0)
        rows_g, gates = gates_of(hop)
        rows = jnp.concatenate([x, gates, dy], axis=0)
        terms, grads = at_home(x, dy, rows_g)
        if last:
            sums = grown(sums, home + [of_partner(*p) for p in partner[:-1]])
        else:
            sent_back([hop], *grads)
        moved_x, moved_dy, rows, terms, grads, dense, sums = lax.optimization_barrier(
            (moved_x, moved_dy, rows, terms, grads, dense, sums)
        )
        block_x, block_dy = moved_x, to_chip(moved_dy, experts, 1, 0) if last else moved_dy
        shared = to_replica(rows, turns[0])
        home.append(terms)
        partner.append((shared[: -dy.shape[0]], shared[-dy.shape[0] :]))
    hop = chips - 1
    summed = other_core(range(hop - 1))
    x = pick_x(hop, (block_x, to_chip(block_x, experts, 0, 1)))
    rows_g, gates = gates_of(hop)
    shared_x = to_replica(jnp.concatenate([x, gates], axis=0), turns[0])
    x, terms, grads = lax.optimization_barrier((x, terms, grads))
    sent_back([hop - 1], *grads)
    sums = grown(sums, [terms, of_partner(*partner[-2])])
    in_grad = summed[1 % chips]
    sums, dense, block_dy, in_grad = lax.optimization_barrier((sums, dense, block_dy, in_grad))

    ring = to_chip(in_grad, experts, 1, 0)
    halves = [pick_dy(hop, 0, block_dy)]
    halves.append(pick_dy(hop, 1, to_chip(block_dy, experts, 0, 1)))
    shared_dy = [to_replica(rows, turns[0]) for rows in halves]
    summed.update(other_core([hop - 1]))
    shared_x, halves, partner[-1], shared_dy[0] = lax.optimization_barrier(
        (shared_x, halves, partner[-1], shared_dy[0])
    )
    terms, grads = at_home(x, jnp.concatenate(halves, axis=0), rows_g)
    sums = grown(sums, [terms, of_partner(*partner[-1])])
    shared_dy, sums = lax.optimization_barrier((shared_dy, sums))

    pairs = pairs_of(of_partner(shared_x, jnp.concatenate(shared_dy, axis=0)))

    def product(m):
        return (sums[0][m] + leaving(pairs[m])).astype(BF16)

    came = [to_replica(product(0), turns[-1])]
    in_grad = plus(ring, summed[2 % chips])
    in_grad, pairs[1:] = lax.optimization_barrier((in_grad, pairs[1:]))
    came.append(to_replica(product(1), turns[-1]))
    gone, grads = lax.optimization_barrier((product(2), grads))
    came.append(to_replica(gone, turns[-1]))
    sent_back([hop], *grads)
    summed.update(other_core([hop]))
    for step in range(3, chips):
        ring = to_chip(in_grad, experts, 1, 0)
        if step == 3:
            came[0], pairs, ring = lax.optimization_barrier((came[0], pairs, ring))
        in_grad = plus(ring, summed[step])
    ring, came[2] = lax.optimization_barrier((to_chip(in_grad, experts, 1, 0), came[2]))
    in_grad = plus(ring, summed[0])
    deltas = []
    for m in range(3):
        total = sums[1][m] + staying(pairs[m]) + came[m].astype(F32)
        for turn in turns[-2:0:-1]:
            size = total.shape[0] // 2
            total = total[:size] + to_replica(total[size:].astype(BF16), turn).astype(F32)
        deltas.append((total / replicas).astype(BF16)[None])
    delta_down, delta_gate, delta_up = deltas
    gate_grad = in_grad[tokens : tokens + top_k, :tokens].T
    return (in_grad[:tokens], gate_grad, delta_gate, delta_up, delta_down)


def solution(mesh):
    by_token = P(("rep", "exp"), None)
    by_expert = P("exp", None, None)
    by_shard = P("exp", "rep", None)
    return jax.shard_map(
        on_device,
        mesh=mesh,
        in_specs=(by_token,) * 4 + (by_expert,) * 3,
        out_specs=(by_token,) * 2 + (by_shard,) * 3,
        check_vma=False,
    )
```

```python
import jax
import jax.numpy as jnp
from jax import lax
from jax.sharding import PartitionSpec as P

F32 = jnp.float32
BF16 = jnp.bfloat16
CORES = 2
EXTRA = 8


def dot_rows(matrix_a, matrix_b):
    return lax.dot_general(
        matrix_a, matrix_b, (((0,), (0,)), ((), ())), preferred_element_type=F32
    )


def dot_last(matrix_a, matrix_b):
    return lax.dot_general(
        matrix_a, matrix_b, (((1,), (1,)), ((), ())), preferred_element_type=F32
    )


def dot_plain(matrix_a, matrix_b):
    return jnp.dot(matrix_a, matrix_b, preferred_element_type=F32)


def to_chip(value, experts, hop, flip):
    chips = experts // CORES
    pairs = [
        (chip * CORES + core, (chip + hop) % chips * CORES + (core ^ flip))
        for chip in range(chips)
        for core in range(CORES)
    ]
    return lax.ppermute(value, "exp", pairs)


def route(meta, top_k, capacity):
    tokens = meta.shape[1]
    hit = meta[:top_k] == lax.axis_index("exp").astype(BF16)
    named = jnp.any(hit, axis=0, keepdims=True)
    gate = jnp.sum(jnp.where(hit, meta[top_k:], 0).astype(F32), axis=0, keepdims=True)
    upto = (jnp.arange(tokens)[:, None] <= jnp.arange(tokens)[None, :]).astype(BF16)
    rank = dot_plain(named.astype(BF16), upto) - 1.0
    chosen = named & (rank == jnp.arange(capacity, dtype=F32)[:, None])
    return hit, chosen, jnp.sum(jnp.where(chosen, gate, 0.0), axis=1, keepdims=True)


def to_replica(value, bit_of_core):
    experts = lax.axis_size("exp")
    pairs = [
        (r * experts + e, (r ^ bit_of_core[e % CORES]) * experts + e)
        for r in range(lax.axis_size("rep"))
        for e in range(experts)
    ]
    return lax.ppermute(value, ("rep", "exp"), pairs)


def on_device(features, out_grad, expert_ids, gate_probs, w_gate, w_up, w_down):
    tokens, model_width = features.shape
    top_k = expert_ids.shape[1]
    experts = lax.axis_size("exp")
    replicas = lax.axis_size("rep")
    chips = experts // CORES
    capacity = min(tokens, 2 * tokens * top_k // experts)
    gate_mat, up_mat, down_mat = (w_gate[0], w_up[0], w_down[0])

    meta = jnp.concatenate([expert_ids.T.astype(BF16), gate_probs.T], axis=0)
    meta = jnp.pad(meta, ((0, EXTRA - 2 * top_k), (0, model_width - tokens)))

    bits = [1 << i for i in range(replicas.bit_length() - 1)]
    turns = list(zip(bits, bits[::-1]))
    own, core = lax.axis_index("rep"), lax.axis_index("exp") % CORES
    shard = model_width // replicas

    def by_shard(rows):
        cut = []
        for i in range(0, replicas, 2):
            masks = [sum(turn[c] for j, turn in enumerate(turns) if i >> j & 1) for c in range(CORES)]
            at = (own ^ jnp.where(core == 0, *masks)) * shard
            cut.append(lax.dynamic_slice_in_dim(rows, at, shard, axis=1))
        return jnp.concatenate(cut, axis=1)

    def expert_rows(x, dy, rows_g):
        pre_gate = dot_plain(x, gate_mat)
        pre_up = dot_plain(x, up_mat)
        gate_sig = jax.nn.sigmoid(pre_gate)
        gate_act = pre_gate * gate_sig
        hidden = (gate_act * pre_up).astype(BF16)
        back_grad = dot_plain(dy, down_mat)
        scaled = (rows_g * dy.astype(F32)).astype(BF16)
        d_hidden = rows_g * back_grad
        d_gate = d_hidden * pre_up * gate_sig * (1.0 + pre_gate * (1.0 - gate_sig))
        d_up = d_hidden * gate_act
        gate_row = jnp.sum(back_grad * hidden.astype(F32), axis=1, keepdims=True).astype(BF16)
        return scaled, hidden, d_gate.astype(BF16), d_up.astype(BF16), gate_row

    routes, dense = {}, {}

    def pick_x(hop, pair):
        rows = []
        for flip in range(CORES):
            named = pair[flip][tokens : tokens + 2 * top_k, :tokens]
            routes[hop, flip] = route(named, top_k, capacity)
            rows.append(dot_plain(routes[hop, flip][1].astype(BF16), pair[flip][:tokens]))
        return jnp.concatenate(rows, axis=0).astype(BF16)

    def pick_dy(hop, flip, block):
        return dot_plain(routes[hop, flip][1].astype(BF16), block).astype(BF16)

    def gates_of(hop):
        rows_g = jnp.concatenate([routes[hop, flip][2] for flip in range(CORES)], axis=0)
        line = rows_g.astype(BF16).T
        return rows_g, jnp.pad(line, ((0, EXTRA - 1), (0, model_width - line.shape[1])))

    def at_home(x, dy, rows_g):
        scaled, hidden, d_gate, d_up, gate_row = expert_rows(x, dy, rows_g)
        return (scaled, x, hidden, d_gate, d_up), (d_gate, d_up, gate_row)

    def of_partner(with_gates, dy):
        rows = dy.shape[0]
        x, rows_g = with_gates[:rows], with_gates[rows : rows + 1, :rows].T.astype(F32)
        scaled, hidden, d_gate, d_up, _ = expert_rows(x, dy, rows_g)
        return scaled, x, hidden, d_gate, d_up

    def sent_back(hops, d_gate, d_up, gate_row):
        row_grad = (dot_last(d_gate, gate_mat) + dot_last(d_up, up_mat)).astype(BF16)
        for place, source in enumerate((hop, flip) for hop in hops for flip in range(CORES)):
            hit, chosen, _ = routes[source]
            mine = slice(place * capacity, (place + 1) * capacity)
            rows = dot_rows(chosen.astype(BF16), row_grad[mine]).astype(BF16)
            value = jnp.where(chosen, gate_row[mine].astype(F32), 0.0)
            gates = jnp.where(hit, jnp.sum(value, axis=0, keepdims=True), 0.0).astype(BF16)
            gates = jnp.pad(gates, ((0, EXTRA - top_k), (0, model_width - tokens)))
            dense[source] = jnp.concatenate([rows, gates], axis=0)

    def joined(groups):
        return [jnp.concatenate(a, axis=0) for a in zip(*groups)]

    kept = max(replicas // 4, 1) * shard

    def pairs_of(terms):
        scaled, x, hidden, d_gate, d_up = terms
        scaled, x = by_shard(scaled), by_shard(x)
        return [(scaled, hidden), (x, d_gate), (x, d_up)]

    def leaving(pair):
        return dot_rows(pair[0][:, kept:], pair[1])

    def staying(pair):
        return dot_rows(pair[0][:, :kept], pair[1])

    def grown(sums, groups):
        pairs = pairs_of(joined(groups))
        gone, stay = [leaving(pair) for pair in pairs], [staying(pair) for pair in pairs]
        if sums:
            gone = [before + after for before, after in zip(sums[0], gone)]
            stay = [before + after for before, after in zip(sums[1], stay)]
        return gone, stay

    def plus(a, b):
        return (a.astype(F32) + b.astype(F32)).astype(BF16)

    def other_core(hops):
        swapped = to_chip(jnp.concatenate([dense[hop, 1] for hop in hops], axis=0), experts, 0, 1)
        return {
            hop: plus(dense[hop, 0], swapped[i * cut : (i + 1) * cut]) for i, hop in enumerate(hops)
        }

    block_dy = out_grad
    other_dy, meta = lax.optimization_barrier((to_chip(out_grad, experts, 0, 1), meta))
    block_x = jnp.concatenate([features, meta], axis=0)
    cut = tokens + EXTRA
    home, partner, sums = [], [], ()
    for hop in range(chips - 1):
        last = hop + 2 == chips
        moved_x = to_chip(block_x, experts, 1, 0)
        moved_dy = block_dy if last else to_chip(block_dy, experts, 1, 0)
        x = pick_x(hop, (block_x, to_chip(block_x, experts, 0, 1)))
        pair_dy = (block_dy, other_dy if hop == 0 else to_chip(block_dy, experts, 0, 1))
        dy = jnp.concatenate([pick_dy(hop, flip, pair_dy[flip]) for flip in range(CORES)], axis=0)
        rows_g, gates = gates_of(hop)
        rows = jnp.concatenate([x, gates, dy], axis=0)
        terms, grads = at_home(x, dy, rows_g)
        if last:
            sums = grown(sums, home + [of_partner(*p) for p in partner[:-1]])
        else:
            sent_back([hop], *grads)
        moved_x, moved_dy, rows, terms, grads, dense, sums = lax.optimization_barrier(
            (moved_x, moved_dy, rows, terms, grads, dense, sums)
        )
        block_x, block_dy = moved_x, to_chip(moved_dy, experts, 1, 0) if last else moved_dy
        shared = to_replica(rows, turns[0])
        home.append(terms)
        partner.append((shared[: -dy.shape[0]], shared[-dy.shape[0] :]))
    hop = chips - 1
    summed = other_core(range(hop - 1))
    x = pick_x(hop, (block_x, to_chip(block_x, experts, 0, 1)))
    rows_g, gates = gates_of(hop)
    shared_x = to_replica(jnp.concatenate([x, gates], axis=0), turns[0])
    x, terms, grads = lax.optimization_barrier((x, terms, grads))
    sent_back([hop - 1], *grads)
    sums = grown(sums, [terms, of_partner(*partner[-2])])
    in_grad = summed[1 % chips]
    sums, dense, block_dy, in_grad = lax.optimization_barrier((sums, dense, block_dy, in_grad))

    ring = to_chip(in_grad, experts, 1, 0)
    halves = [pick_dy(hop, 0, block_dy)]
    halves.append(pick_dy(hop, 1, to_chip(block_dy, experts, 0, 1)))
    shared_dy = [to_replica(rows, turns[0]) for rows in halves]
    summed.update(other_core([hop - 1]))
    shared_x, halves, partner[-1], shared_dy[0] = lax.optimization_barrier(
        (shared_x, halves, partner[-1], shared_dy[0])
    )
    terms, grads = at_home(x, jnp.concatenate(halves, axis=0), rows_g)
    sums = grown(sums, [terms, of_partner(*partner[-1])])
    shared_dy, sums = lax.optimization_barrier((shared_dy, sums))

    pairs = pairs_of(of_partner(shared_x, jnp.concatenate(shared_dy, axis=0)))

    def product(m):
        return (sums[0][m] + leaving(pairs[m])).astype(BF16)

    came = [to_replica(product(0), turns[-1])]
    ring, pairs[1:] = lax.optimization_barrier((ring, pairs[1:]))
    in_grad = plus(ring, summed[2 % chips])
    came.append(to_replica(product(1), turns[-1]))
    gone, grads = lax.optimization_barrier((product(2), grads))
    came.append(to_replica(gone, turns[-1]))
    sent_back([hop], *grads)
    summed.update(other_core([hop]))
    for step in range(3, chips):
        ring = to_chip(in_grad, experts, 1, 0)
        if step == 3:
            came[0], pairs, ring = lax.optimization_barrier((came[0], pairs, ring))
        in_grad = plus(ring, summed[step])
    ring, came[2] = lax.optimization_barrier((to_chip(in_grad, experts, 1, 0), came[2]))
    in_grad = plus(ring, summed[0])
    deltas = []
    for m in range(3):
        total = sums[1][m] + staying(pairs[m]) + came[m].astype(F32)
        for turn in turns[-2:0:-1]:
            size = total.shape[0] // 2
            total = total[:size] + to_replica(total[size:].astype(BF16), turn).astype(F32)
        deltas.append((total / replicas).astype(BF16)[None])
    delta_down, delta_gate, delta_up = deltas
    gate_grad = in_grad[tokens : tokens + top_k, :tokens].T
    return (in_grad[:tokens], gate_grad, delta_gate, delta_up, delta_down)


def solution(mesh):
    by_token = P(("rep", "exp"), None)
    by_expert = P("exp", None, None)
    by_shard = P("exp", "rep", None)
    return jax.shard_map(
        on_device,
        mesh=mesh,
        in_specs=(by_token,) * 4 + (by_expert,) * 3,
        out_specs=(by_token,) * 2 + (by_shard,) * 3,
        check_vma=False,
    )
```

```python
import jax
import jax.numpy as jnp
from jax import lax
from jax.sharding import PartitionSpec as P

F32 = jnp.float32
BF16 = jnp.bfloat16
CORES = 2
EXTRA = 8


def dot_rows(matrix_a, matrix_b):
    return lax.dot_general(
        matrix_a, matrix_b, (((0,), (0,)), ((), ())), preferred_element_type=F32
    )


def dot_last(matrix_a, matrix_b):
    return lax.dot_general(
        matrix_a, matrix_b, (((1,), (1,)), ((), ())), preferred_element_type=F32
    )


def dot_plain(matrix_a, matrix_b):
    return jnp.dot(matrix_a, matrix_b, preferred_element_type=F32)


def to_chip(value, experts, hop, flip):
    chips = experts // CORES
    pairs = [
        (chip * CORES + core, (chip + hop) % chips * CORES + (core ^ flip))
        for chip in range(chips)
        for core in range(CORES)
    ]
    return lax.ppermute(value, "exp", pairs)


def route(meta, top_k, capacity):
    tokens = meta.shape[1]
    hit = meta[:top_k] == lax.axis_index("exp").astype(BF16)
    named = jnp.any(hit, axis=0, keepdims=True)
    gate = jnp.sum(jnp.where(hit, meta[top_k:], 0).astype(F32), axis=0, keepdims=True)
    upto = (jnp.arange(tokens)[:, None] <= jnp.arange(tokens)[None, :]).astype(BF16)
    rank = dot_plain(named.astype(BF16), upto) - 1.0
    chosen = named & (rank == jnp.arange(capacity, dtype=F32)[:, None])
    return hit, chosen, jnp.sum(jnp.where(chosen, gate, 0.0), axis=1, keepdims=True)


def to_replica(value, bit_of_core):
    experts = lax.axis_size("exp")
    pairs = [
        (r * experts + e, (r ^ bit_of_core[e % CORES]) * experts + e)
        for r in range(lax.axis_size("rep"))
        for e in range(experts)
    ]
    return lax.ppermute(value, ("rep", "exp"), pairs)


def on_device(features, out_grad, expert_ids, gate_probs, w_gate, w_up, w_down):
    tokens, model_width = features.shape
    top_k = expert_ids.shape[1]
    experts = lax.axis_size("exp")
    replicas = lax.axis_size("rep")
    chips = experts // CORES
    capacity = min(tokens, 2 * tokens * top_k // experts)
    gate_mat, up_mat, down_mat = (w_gate[0], w_up[0], w_down[0])

    meta = jnp.concatenate([expert_ids.T.astype(BF16), gate_probs.T], axis=0)
    meta = jnp.pad(meta, ((0, EXTRA - 2 * top_k), (0, model_width - tokens)))

    bits = [1 << i for i in range(replicas.bit_length() - 1)]
    turns = list(zip(bits, bits[::-1]))
    own, core = lax.axis_index("rep"), lax.axis_index("exp") % CORES
    shard = model_width // replicas

    def by_shard(rows):
        cut = []
        for i in range(0, replicas, 2):
            masks = [sum(turn[c] for j, turn in enumerate(turns) if i >> j & 1) for c in range(CORES)]
            at = (own ^ jnp.where(core == 0, *masks)) * shard
            cut.append(lax.dynamic_slice_in_dim(rows, at, shard, axis=1))
        return jnp.concatenate(cut, axis=1)

    def expert_rows(x, dy, rows_g):
        pre_gate = dot_plain(x, gate_mat)
        pre_up = dot_plain(x, up_mat)
        gate_sig = jax.nn.sigmoid(pre_gate)
        gate_act = pre_gate * gate_sig
        hidden = (gate_act * pre_up).astype(BF16)
        back_grad = dot_plain(dy, down_mat)
        scaled = (rows_g * dy.astype(F32)).astype(BF16)
        d_hidden = rows_g * back_grad
        d_gate = d_hidden * pre_up * gate_sig * (1.0 + pre_gate * (1.0 - gate_sig))
        d_up = d_hidden * gate_act
        gate_row = jnp.sum(back_grad * hidden.astype(F32), axis=1, keepdims=True).astype(BF16)
        return scaled, hidden, d_gate.astype(BF16), d_up.astype(BF16), gate_row

    routes, dense = {}, {}

    def pick_x(hop, pair):
        rows = []
        for flip in range(CORES):
            named = pair[flip][tokens : tokens + 2 * top_k, :tokens]
            routes[hop, flip] = route(named, top_k, capacity)
            rows.append(dot_plain(routes[hop, flip][1].astype(BF16), pair[flip][:tokens]))
        return jnp.concatenate(rows, axis=0).astype(BF16)

    def pick_dy(hop, flip, block):
        return dot_plain(routes[hop, flip][1].astype(BF16), block).astype(BF16)

    def gates_of(hop):
        rows_g = jnp.concatenate([routes[hop, flip][2] for flip in range(CORES)], axis=0)
        line = rows_g.astype(BF16).T
        return rows_g, jnp.pad(line, ((0, EXTRA - 1), (0, model_width - line.shape[1])))

    def at_home(x, dy, rows_g):
        scaled, hidden, d_gate, d_up, gate_row = expert_rows(x, dy, rows_g)
        return (scaled, x, hidden, d_gate, d_up), (d_gate, d_up, gate_row)

    def of_partner(with_gates, dy):
        rows = dy.shape[0]
        x, rows_g = with_gates[:rows], with_gates[rows : rows + 1, :rows].T.astype(F32)
        scaled, hidden, d_gate, d_up, _ = expert_rows(x, dy, rows_g)
        return scaled, x, hidden, d_gate, d_up

    def sent_back(hops, d_gate, d_up, gate_row):
        row_grad = (dot_last(d_gate, gate_mat) + dot_last(d_up, up_mat)).astype(BF16)
        for place, source in enumerate((hop, flip) for hop in hops for flip in range(CORES)):
            hit, chosen, _ = routes[source]
            mine = slice(place * capacity, (place + 1) * capacity)
            rows = dot_rows(chosen.astype(BF16), row_grad[mine]).astype(BF16)
            value = jnp.where(chosen, gate_row[mine].astype(F32), 0.0)
            gates = jnp.where(hit, jnp.sum(value, axis=0, keepdims=True), 0.0).astype(BF16)
            gates = jnp.pad(gates, ((0, EXTRA - top_k), (0, model_width - tokens)))
            dense[source] = jnp.concatenate([rows, gates], axis=0)

    def joined(groups):
        return [jnp.concatenate(a, axis=0) for a in zip(*groups)]

    kept = max(replicas // 4, 1) * shard

    def pairs_of(terms):
        scaled, x, hidden, d_gate, d_up = terms
        scaled, x = by_shard(scaled), by_shard(x)
        return [(scaled, hidden), (x, d_gate), (x, d_up)]

    def leaving(pair):
        return dot_rows(pair[0][:, kept:], pair[1])

    def staying(pair):
        return dot_rows(pair[0][:, :kept], pair[1])

    def grown(sums, groups):
        pairs = pairs_of(joined(groups))
        gone, stay = [leaving(pair) for pair in pairs], [staying(pair) for pair in pairs]
        if sums:
            gone = [before + after for before, after in zip(sums[0], gone)]
            stay = [before + after for before, after in zip(sums[1], stay)]
        return gone, stay

    def plus(a, b):
        return (a.astype(F32) + b.astype(F32)).astype(BF16)

    def other_core(hops):
        swapped = to_chip(jnp.concatenate([dense[hop, 1] for hop in hops], axis=0), experts, 0, 1)
        return {
            hop: plus(dense[hop, 0], swapped[i * cut : (i + 1) * cut]) for i, hop in enumerate(hops)
        }

    block_dy = out_grad
    other_dy, meta = lax.optimization_barrier((to_chip(out_grad, experts, 0, 1), meta))
    block_x = jnp.concatenate([features, meta], axis=0)
    cut = tokens + EXTRA
    home, partner, sums = [], [], ()
    for hop in range(chips - 1):
        last = hop + 2 == chips
        moved_x = to_chip(block_x, experts, 1, 0)
        moved_dy = block_dy if last else to_chip(block_dy, experts, 1, 0)
        x = pick_x(hop, (block_x, to_chip(block_x, experts, 0, 1)))
        pair_dy = (block_dy, other_dy if hop == 0 else to_chip(block_dy, experts, 0, 1))
        dy = jnp.concatenate([pick_dy(hop, flip, pair_dy[flip]) for flip in range(CORES)], axis=0)
        rows_g, gates = gates_of(hop)
        rows = jnp.concatenate([x, gates, dy], axis=0)
        terms, grads = at_home(x, dy, rows_g)
        if last:
            sums = grown(sums, home + [of_partner(*p) for p in partner[:-1]])
        else:
            sent_back([hop], *grads)
        moved_x, moved_dy, rows, terms, grads, dense, sums = lax.optimization_barrier(
            (moved_x, moved_dy, rows, terms, grads, dense, sums)
        )
        block_x, block_dy = moved_x, to_chip(moved_dy, experts, 1, 0) if last else moved_dy
        shared = to_replica(rows, turns[0])
        home.append(terms)
        partner.append((shared[: -dy.shape[0]], shared[-dy.shape[0] :]))
    hop = chips - 1
    summed = other_core(range(hop - 1))
    x = pick_x(hop, (block_x, to_chip(block_x, experts, 0, 1)))
    rows_g, gates = gates_of(hop)
    shared_x = to_replica(jnp.concatenate([x, gates], axis=0), turns[0])
    x, terms, grads = lax.optimization_barrier((x, terms, grads))
    sent_back([hop - 1], *grads)
    sums = grown(sums, [terms, of_partner(*partner[-2])])
    in_grad = summed[1 % chips]
    sums, dense, block_dy, in_grad = lax.optimization_barrier((sums, dense, block_dy, in_grad))

    ring = to_chip(in_grad, experts, 1, 0)
    halves = [pick_dy(hop, 0, block_dy)]
    other_dy, partner[-1] = lax.optimization_barrier((to_chip(block_dy, experts, 0, 1), partner[-1]))
    halves.append(pick_dy(hop, 1, other_dy))
    shared_dy = [to_replica(rows, turns[0]) for rows in halves]
    summed.update(other_core([hop - 1]))
    shared_x, halves, shared_dy[0] = lax.optimization_barrier((shared_x, halves, shared_dy[0]))
    terms, grads = at_home(x, jnp.concatenate(halves, axis=0), rows_g)
    sums = grown(sums, [terms, of_partner(*partner[-1])])
    shared_dy, sums = lax.optimization_barrier((shared_dy, sums))

    pairs = pairs_of(of_partner(shared_x, jnp.concatenate(shared_dy, axis=0)))

    def product(m):
        return (sums[0][m] + leaving(pairs[m])).astype(BF16)

    came = [to_replica(product(0), turns[-1])]
    ring, pairs[1:] = lax.optimization_barrier((ring, pairs[1:]))
    in_grad = plus(ring, summed[2 % chips])
    came.append(to_replica(product(1), turns[-1]))
    gone, grads = lax.optimization_barrier((product(2), grads))
    came.append(to_replica(gone, turns[-1]))
    sent_back([hop], *grads)
    summed.update(other_core([hop]))
    for step in range(3, chips):
        ring = to_chip(in_grad, experts, 1, 0)
        if step == 3:
            came[0], pairs, ring = lax.optimization_barrier((came[0], pairs, ring))
        in_grad = plus(ring, summed[step])
    ring, came[2] = lax.optimization_barrier((to_chip(in_grad, experts, 1, 0), came[2]))
    in_grad = plus(ring, summed[0])
    deltas = []
    for m in range(3):
        total = sums[1][m] + staying(pairs[m]) + came[m].astype(F32)
        for turn in turns[-2:0:-1]:
            size = total.shape[0] // 2
            total = total[:size] + to_replica(total[size:].astype(BF16), turn).astype(F32)
        deltas.append((total / replicas).astype(BF16)[None])
    delta_down, delta_gate, delta_up = deltas
    gate_grad = in_grad[tokens : tokens + top_k, :tokens].T
    return (in_grad[:tokens], gate_grad, delta_gate, delta_up, delta_down)


def solution(mesh):
    by_token = P(("rep", "exp"), None)
    by_expert = P("exp", None, None)
    by_shard = P("exp", "rep", None)
    return jax.shard_map(
        on_device,
        mesh=mesh,
        in_specs=(by_token,) * 4 + (by_expert,) * 3,
        out_specs=(by_token,) * 2 + (by_shard,) * 3,
        check_vma=False,
    )
```

```python
import jax
import jax.numpy as jnp
from jax import lax
from jax.sharding import PartitionSpec as P

F32 = jnp.float32
BF16 = jnp.bfloat16
CORES = 2
EXTRA = 8


def dot_rows(matrix_a, matrix_b):
    return lax.dot_general(
        matrix_a, matrix_b, (((0,), (0,)), ((), ())), preferred_element_type=F32
    )


def dot_last(matrix_a, matrix_b):
    return lax.dot_general(
        matrix_a, matrix_b, (((1,), (1,)), ((), ())), preferred_element_type=F32
    )


def dot_plain(matrix_a, matrix_b):
    return jnp.dot(matrix_a, matrix_b, preferred_element_type=F32)


def to_chip(value, experts, hop, flip):
    chips = experts // CORES
    pairs = [
        (chip * CORES + core, (chip + hop) % chips * CORES + (core ^ flip))
        for chip in range(chips)
        for core in range(CORES)
    ]
    return lax.ppermute(value, "exp", pairs)


def route(meta, top_k, capacity):
    tokens = meta.shape[1]
    hit = meta[:top_k] == lax.axis_index("exp").astype(BF16)
    named = jnp.any(hit, axis=0, keepdims=True)
    gate = jnp.sum(jnp.where(hit, meta[top_k:], 0).astype(F32), axis=0, keepdims=True)
    upto = (jnp.arange(tokens)[:, None] <= jnp.arange(tokens)[None, :]).astype(BF16)
    rank = dot_plain(named.astype(BF16), upto) - 1.0
    chosen = named & (rank == jnp.arange(capacity, dtype=F32)[:, None])
    return hit, chosen, jnp.sum(jnp.where(chosen, gate, 0.0), axis=1, keepdims=True)


def to_replica(value, bit_of_core):
    experts = lax.axis_size("exp")
    pairs = [
        (r * experts + e, (r ^ bit_of_core[e % CORES]) * experts + e)
        for r in range(lax.axis_size("rep"))
        for e in range(experts)
    ]
    return lax.ppermute(value, ("rep", "exp"), pairs)


def on_device(features, out_grad, expert_ids, gate_probs, w_gate, w_up, w_down):
    tokens, model_width = features.shape
    top_k = expert_ids.shape[1]
    experts = lax.axis_size("exp")
    replicas = lax.axis_size("rep")
    chips = experts // CORES
    capacity = min(tokens, 2 * tokens * top_k // experts)
    gate_mat, up_mat, down_mat = (w_gate[0], w_up[0], w_down[0])

    meta = jnp.concatenate([expert_ids.T.astype(BF16), gate_probs.T], axis=0)
    meta = jnp.pad(meta, ((0, EXTRA - 2 * top_k), (0, model_width - tokens)))

    bits = [1 << i for i in range(replicas.bit_length() - 1)]
    turns = list(zip(bits, bits[::-1]))
    own, core = lax.axis_index("rep"), lax.axis_index("exp") % CORES
    shard = model_width // replicas

    def by_shard(rows):
        cut = []
        for i in range(0, replicas, 2):
            masks = [sum(turn[c] for j, turn in enumerate(turns) if i >> j & 1) for c in range(CORES)]
            at = (own ^ jnp.where(core == 0, *masks)) * shard
            cut.append(lax.dynamic_slice_in_dim(rows, at, shard, axis=1))
        return jnp.concatenate(cut, axis=1)

    def expert_rows(x, dy, rows_g):
        pre_gate = dot_plain(x, gate_mat)
        pre_up = dot_plain(x, up_mat)
        gate_sig = jax.nn.sigmoid(pre_gate)
        gate_act = pre_gate * gate_sig
        hidden = (gate_act * pre_up).astype(BF16)
        back_grad = dot_plain(dy, down_mat)
        scaled = (rows_g * dy.astype(F32)).astype(BF16)
        d_hidden = rows_g * back_grad
        d_gate = d_hidden * pre_up * gate_sig * (1.0 + pre_gate * (1.0 - gate_sig))
        d_up = d_hidden * gate_act
        gate_row = jnp.sum(back_grad * hidden.astype(F32), axis=1, keepdims=True).astype(BF16)
        return scaled, hidden, d_gate.astype(BF16), d_up.astype(BF16), gate_row

    routes, dense = {}, {}

    def pick_x(hop, pair):
        rows = []
        for flip in range(CORES):
            named = pair[flip][tokens : tokens + 2 * top_k, :tokens]
            routes[hop, flip] = route(named, top_k, capacity)
            rows.append(dot_plain(routes[hop, flip][1].astype(BF16), pair[flip][:tokens]))
        return jnp.concatenate(rows, axis=0).astype(BF16)

    def pick_dy(hop, flip, block):
        return dot_plain(routes[hop, flip][1].astype(BF16), block).astype(BF16)

    def gates_of(hop):
        rows_g = jnp.concatenate([routes[hop, flip][2] for flip in range(CORES)], axis=0)
        line = rows_g.astype(BF16).T
        return rows_g, jnp.pad(line, ((0, EXTRA - 1), (0, model_width - line.shape[1])))

    def at_home(x, dy, rows_g):
        scaled, hidden, d_gate, d_up, gate_row = expert_rows(x, dy, rows_g)
        return (scaled, x, hidden, d_gate, d_up), (d_gate, d_up, gate_row)

    def of_partner(with_gates, dy):
        rows = dy.shape[0]
        x, rows_g = with_gates[:rows], with_gates[rows : rows + 1, :rows].T.astype(F32)
        scaled, hidden, d_gate, d_up, _ = expert_rows(x, dy, rows_g)
        return scaled, x, hidden, d_gate, d_up

    def sent_back(hops, d_gate, d_up, gate_row):
        row_grad = (dot_last(d_gate, gate_mat) + dot_last(d_up, up_mat)).astype(BF16)
        for place, source in enumerate((hop, flip) for hop in hops for flip in range(CORES)):
            hit, chosen, _ = routes[source]
            mine = slice(place * capacity, (place + 1) * capacity)
            rows = dot_rows(chosen.astype(BF16), row_grad[mine]).astype(BF16)
            value = jnp.where(chosen, gate_row[mine].astype(F32), 0.0)
            gates = jnp.where(hit, jnp.sum(value, axis=0, keepdims=True), 0.0).astype(BF16)
            gates = jnp.pad(gates, ((0, EXTRA - top_k), (0, model_width - tokens)))
            dense[source] = jnp.concatenate([rows, gates], axis=0)

    def joined(groups):
        return [jnp.concatenate(a, axis=0) for a in zip(*groups)]

    kept = max(replicas // 4, 1) * shard

    def pairs_of(terms):
        scaled, x, hidden, d_gate, d_up = terms
        scaled, x = by_shard(scaled), by_shard(x)
        return [(scaled, hidden), (x, d_gate), (x, d_up)]

    def leaving(pair):
        return dot_rows(pair[0][:, kept:], pair[1])

    def staying(pair):
        return dot_rows(pair[0][:, :kept], pair[1])

    def grown(sums, groups):
        pairs = pairs_of(joined(groups))
        gone, stay = [leaving(pair) for pair in pairs], [staying(pair) for pair in pairs]
        if sums:
            gone = [before + after for before, after in zip(sums[0], gone)]
            stay = [before + after for before, after in zip(sums[1], stay)]
        return gone, stay

    def plus(a, b):
        return (a.astype(F32) + b.astype(F32)).astype(BF16)

    def other_core(hops):
        swapped = to_chip(jnp.concatenate([dense[hop, 1] for hop in hops], axis=0), experts, 0, 1)
        return {
            hop: plus(dense[hop, 0], swapped[i * cut : (i + 1) * cut]) for i, hop in enumerate(hops)
        }

    block_dy = out_grad
    other_dy, meta = lax.optimization_barrier((to_chip(out_grad, experts, 0, 1), meta))
    block_x = jnp.concatenate([features, meta], axis=0)
    cut = tokens + EXTRA
    home, partner, sums = [], [], ()
    for hop in range(chips - 1):
        last = hop + 2 == chips
        moved_x = to_chip(block_x, experts, 1, 0)
        moved_dy = block_dy if last else to_chip(block_dy, experts, 1, 0)
        x = pick_x(hop, (block_x, to_chip(block_x, experts, 0, 1)))
        pair_dy = (block_dy, other_dy if hop == 0 else to_chip(block_dy, experts, 0, 1))
        dy = jnp.concatenate([pick_dy(hop, flip, pair_dy[flip]) for flip in range(CORES)], axis=0)
        rows_g, gates = gates_of(hop)
        rows = jnp.concatenate([x, gates, dy], axis=0)
        terms, grads = at_home(x, dy, rows_g)
        if last:
            sums = grown(sums, home + [of_partner(*p) for p in partner[:-1]])
        else:
            sent_back([hop], *grads)
        moved_x, moved_dy, rows, terms, grads, dense, sums = lax.optimization_barrier(
            (moved_x, moved_dy, rows, terms, grads, dense, sums)
        )
        block_x, block_dy = moved_x, to_chip(moved_dy, experts, 1, 0) if last else moved_dy
        shared = to_replica(rows, turns[0])
        home.append(terms)
        partner.append((shared[: -dy.shape[0]], shared[-dy.shape[0] :]))
    hop = chips - 1
    summed = other_core(range(hop - 1))
    x = pick_x(hop, (block_x, to_chip(block_x, experts, 0, 1)))
    rows_g, gates = gates_of(hop)
    shared_x = to_replica(jnp.concatenate([x, gates], axis=0), turns[0])
    x, terms, grads = lax.optimization_barrier((x, terms, grads))
    sent_back([hop - 1], *grads)
    sums = grown(sums, [terms, of_partner(*partner[-2])])
    in_grad = summed[1 % chips]
    sums, dense, block_dy, in_grad = lax.optimization_barrier((sums, dense, block_dy, in_grad))

    ring = to_chip(in_grad, experts, 1, 0)
    halves = [pick_dy(hop, 0, block_dy)]
    halves.append(pick_dy(hop, 1, to_chip(block_dy, experts, 0, 1)))
    shared_dy = [to_replica(rows, turns[0]) for rows in halves]
    summed.update(other_core([hop - 1]))
    shared_x, halves, partner[-1], shared_dy[0] = lax.optimization_barrier(
        (shared_x, halves, partner[-1], shared_dy[0])
    )
    terms, grads = at_home(x, jnp.concatenate(halves, axis=0), rows_g)
    sums = grown(sums, [terms, of_partner(*partner[-1])])
    shared_dy, sums = lax.optimization_barrier((shared_dy, sums))

    pairs = pairs_of(of_partner(shared_x, jnp.concatenate(shared_dy, axis=0)))

    def product(m):
        return (sums[0][m] + leaving(pairs[m])).astype(BF16)

    came = [to_replica(product(0), turns[-1])]
    ring, pairs[1:] = lax.optimization_barrier((ring, pairs[1:]))
    in_grad = plus(ring, summed[2 % chips])
    came.append(to_replica(product(1), turns[-1]))
    gone, grads = lax.optimization_barrier((product(2), grads))
    came.append(to_replica(gone, turns[-1]))
    sent_back([hop], *grads)
    summed.update(other_core([hop]))
    for step in range(3, chips):
        ring = to_chip(in_grad, experts, 1, 0)
        if step == 3:
            came[0], pairs, ring = lax.optimization_barrier((came[0], pairs, ring))
        in_grad = plus(ring, summed[step])
    ring, came[2] = lax.optimization_barrier((to_chip(in_grad, experts, 1, 0), came[2]))
    in_grad = plus(ring[:tokens], summed[0][:tokens])
    gate_grad = plus(ring[tokens : tokens + top_k, :tokens], summed[0][tokens : tokens + top_k, :tokens]).T
    deltas = []
    for m in range(3):
        total = sums[1][m] + staying(pairs[m]) + came[m].astype(F32)
        for turn in turns[-2:0:-1]:
            size = total.shape[0] // 2
            total = total[:size] + to_replica(total[size:].astype(BF16), turn).astype(F32)
        deltas.append((total / replicas).astype(BF16)[None])
    delta_down, delta_gate, delta_up = deltas
    return (in_grad, gate_grad, delta_gate, delta_up, delta_down)


def solution(mesh):
    by_token = P(("rep", "exp"), None)
    by_expert = P("exp", None, None)
    by_shard = P("exp", "rep", None)
    return jax.shard_map(
        on_device,
        mesh=mesh,
        in_specs=(by_token,) * 4 + (by_expert,) * 3,
        out_specs=(by_token,) * 2 + (by_shard,) * 3,
        check_vma=False,
    )
```
